128 devices in a mesh: gossip: 8 (over x, z_hi), fsdp: 2 (over z_lo), tensor: 8 (over y, core).
Axes of the slice: x: 4, y: 4, z: 4 (z_hi: 2, z_lo: 2; z = z_hi * 2 + z_lo), core: 2. Of those that a mesh axis runs over, the one named last changes fastest.
Arguments:
- normed: bfloat16 [8192, 8192], P(('gossip', 'fsdp', 'tensor')), may hold values from -24 to 24
- key_cotangent: bfloat16 [8192, 1024], P(('gossip', 'fsdp'), 'tensor'), may hold values from -6 to 6
- value_cotangent: bfloat16 [8192, 1024], P(('gossip', 'fsdp'), 'tensor'), may hold values from -6 to 6
- key_weight: float32 [8, 8192, 1024], P('gossip', 'fsdp', 'tensor'), may hold values from -6 to 6
- value_weight: float32 [8, 8192, 1024], P('gossip', 'fsdp', 'tensor'), may hold values from -6 to 6
- key_momentum: float32 [8, 8192, 1024], P('gossip', 'fsdp', 'tensor'), may hold values from -6 to 6
- value_momentum: float32 [8, 8192, 1024], P('gossip', 'fsdp', 'tensor'), may hold values from -6 to 6
- step_index: int32 [], replicated, may hold values from 0 to 2999
Outputs:
- projected_keys: bfloat16 [8192, 1024], P(('gossip', 'fsdp'), 'tensor')
- projected_values: bfloat16 [8192, 1024], P(('gossip', 'fsdp'), 'tensor')
- input_grad: bfloat16 [8192, 8192], P(('gossip', 'fsdp', 'tensor'))
- new_key_weight: float32 [8, 8192, 1024], P('gossip', 'fsdp', 'tensor')
- new_value_weight: float32 [8, 8192, 1024], P('gossip', 'fsdp', 'tensor')
- new_key_momentum: float32 [8, 8192, 1024], P('gossip', 'fsdp', 'tensor')
- new_value_momentum: float32 [8, 8192, 1024], P('gossip', 'fsdp', 'tensor')
The draws below stay inside these ranges and needn't reach their ends.
All inputs are finite; a program needn't handle non-finite values.
Results may differ from the reference program's by a relative error of at most 0.0055.
Values may be sent and summed in bfloat16 or wider, within the bound.
No kernel may reach another device: no remote copies, remote signals or barrier semaphores. Data moves between devices by JAX's collectives and lax.ppermute only.
A program may use at most 192 MiB of HBM per device.

```python
import jax
import jax.numpy as jnp
from jax import lax

D = 8192
TOK_DEV = 512
KVW = 1024
REPLICAS = 8
TOKENS = 8192
N_GOSSIP = 8
N_FSDP = 2


def raised(array, stream_key, source, target, blocks, factor):
    owner, partner = [(jnp.arange(array.shape[axis_at]) // (array.shape[axis_at] // blocks)).reshape([-1 if axis == axis_at else 1 for axis in range(array.ndim)]) for axis_at in (source, target)]
    chosen = jax.random.permutation(stream_key, blocks)[partner]
    strong = (owner == chosen) | (owner == (partner + blocks // 2) % blocks)
    return jnp.where(strong, factor * array, array)


def level_of(stream_key, dims, pieces, low, high):
    gain, own = 1.0, jax.random.fold_in(stream_key, 6)
    for dim, parts in pieces:
        heights = jnp.exp(jax.random.uniform(jax.random.fold_in(own, dim), (parts,), jnp.float32, low / len(pieces), high / len(pieces)))
        gain = gain * jnp.repeat(heights, dims[dim] // parts).reshape([-1 if axis == dim else 1 for axis in range(len(dims))])
    return gain


def centred(stream_key, shape, spread, bound, pieces=(), held_as=jnp.bfloat16):
    array = spread * jax.random.normal(stream_key, shape, jnp.float32)
    if pieces:
        array = array * level_of(stream_key, shape, pieces, -0.22, 0.18)
    return jnp.clip(array, -bound, bound).astype(held_as)


def bell_draw_with(rng, dims, spread, most, split, heavy, held_as=jnp.bfloat16):
    values = spread * jax.random.normal(rng, dims, jnp.float32)
    if split:
        values = values * level_of(rng, dims, split, -0.22, 0.18)
    return jnp.clip(raised(values, jax.random.fold_in(rng, 3), *heavy), -most, most).astype(held_as)


def setup_inputs(seed: int = 0) -> dict:
    key_of = jax.random.split(jax.random.key(seed), 9)
    return {
        "normed": bell_draw_with(key_of[0], (TOKENS, D), 1.0, 24.0, ((0, 128),), (0, 1, 128, 5.5)),
        "key_cotangent": centred(key_of[1], (TOKENS, KVW), 1.0, 6.0, ((0, 16), (1, 8))),
        "value_cotangent": centred(key_of[2], (TOKENS, KVW), 1.0, 6.0, ((0, 16), (1, 8))),
        "key_weight": centred(key_of[3], (REPLICAS, D, KVW), 1.0, 6.0, ((0, 8), (1, 2), (2, 8)), jnp.float32),
        "value_weight": centred(key_of[4], (REPLICAS, D, KVW), 1.0, 6.0, ((0, 8), (1, 2), (2, 8)), jnp.float32),
        "key_momentum": centred(key_of[5], (REPLICAS, D, KVW), 1.0, 6.0, ((0, 8), (1, 2), (2, 8)), jnp.float32),
        "value_momentum": centred(key_of[6], (REPLICAS, D, KVW), 1.0, 6.0, ((0, 8), (1, 2), (2, 8)), jnp.float32),
        "step_index": jax.random.randint(key_of[7], (), 0, 3000).astype(jnp.int32),
    }


momentum_decay = 0.9
learn_rate = 0.5


def reference(normed, key_cotangent, value_cotangent, key_weight, value_weight, key_momentum, value_momentum, step_index):
    per_replica = TOK_DEV * N_FSDP
    scaling = D ** -0.5
    key_list = []
    value_list = []
    input_list = []
    key_grads = []
    value_grads = []
    contract = (((0,), (0,)), ((), ()))
    for member in range(N_GOSSIP):
        token_rows = normed[member * per_replica:(member + 1) * per_replica]
        key_part = key_cotangent[member * per_replica:(member + 1) * per_replica]
        value_part = value_cotangent[member * per_replica:(member + 1) * per_replica]
        key_bf = key_weight[member].astype(jnp.bfloat16)
        value_bf = value_weight[member].astype(jnp.bfloat16)
        key_list.append((jnp.dot(token_rows, key_bf, preferred_element_type=jnp.float32) * scaling).astype(jnp.bfloat16))
        value_list.append((jnp.dot(token_rows, value_bf, preferred_element_type=jnp.float32) * scaling).astype(jnp.bfloat16))
        key_grads.append(lax.dot_general(token_rows, key_part, contract, preferred_element_type=jnp.float32) * scaling)
        value_grads.append(lax.dot_general(token_rows, value_part, contract, preferred_element_type=jnp.float32) * scaling)
        backward = jnp.dot(key_part, key_bf.T, preferred_element_type=jnp.float32) + jnp.dot(value_part, value_bf.T, preferred_element_type=jnp.float32)
        input_list.append((backward * scaling).astype(jnp.bfloat16))
    new_key_momentum = momentum_decay * key_momentum + jnp.stack(key_grads)
    new_value_momentum = momentum_decay * value_momentum + jnp.stack(value_grads)
    moved_key = key_weight - learn_rate * new_key_momentum
    moved_value = value_weight - learn_rate * new_value_momentum
    levels = N_GOSSIP.bit_length() - 1
    bit_number = (step_index % levels).astype(jnp.int32)
    shifted = jnp.left_shift(jnp.int32(1), bit_number).astype(jnp.int32)
    partner = jnp.bitwise_xor(jnp.arange(N_GOSSIP, dtype=jnp.int32), shifted).astype(jnp.int32)
    new_key_weight = 0.5 * (moved_key + jnp.take(moved_key, partner, axis=0))
    new_value_weight = 0.5 * (moved_value + jnp.take(moved_value, partner, axis=0))
    return (jnp.concatenate(key_list, axis=0), jnp.concatenate(value_list, axis=0), jnp.concatenate(input_list, axis=0), new_key_weight, new_value_weight, new_key_momentum, new_value_momentum)
```

```python
from functools import partial

import jax
import jax.numpy as jnp
from jax import lax
from jax.experimental import pallas as pl
from jax.experimental.pallas import tpu as pltpu
from jax.sharding import PartitionSpec as P

D = 8192
SCALING = D ** (-0.5)
momentum_decay = 0.9
learn_rate = 0.5

F32 = jnp.float32
BF = jnp.bfloat16
HALF = 4096
QUARTER = 2048
CHUNKS = 2
CH = QUARTER // CHUNKS
ROWS = 64
TOK = 512
COLS = 128
TILE = 512

MB = 1024 * 1024


def sds(shape, dtype):
    return jax.ShapeDtypeStruct(shape, dtype)


def params(mib):
    return pltpu.CompilerParams(vmem_limit_bytes=mib * MB)


def cost(flops, nbytes):
    return pl.CostEstimate(flops=flops, bytes_accessed=nbytes, transcendentals=0)


def smem():
    return pl.BlockSpec(memory_space=pltpu.SMEM)


def vmem():
    return pl.BlockSpec(memory_space=pltpu.VMEM)


def split_kernel(where, x, k, v, kv, *outs):
    f, c = where[0], where[2]
    kv[:, :COLS] = k[...]
    kv[:, COLS:] = v[...]
    quarters = (2 * f + c, 2 * f + 1 - c, 2 * (1 - f) + c, 2 * (1 - f) + 1 - c)
    at = 0
    for q in quarters:
        for h in range(CHUNKS):
            start = pl.multiple_of(q * QUARTER + h * CH, CH)
            outs[at][...] = x[:, pl.ds(start, CH)]
            at += 1


def split_inputs(where, x, k, v):
    piece = sds((ROWS, CH), BF)
    out = pl.pallas_call(
        split_kernel,
        out_shape=[sds((TOK, 2 * COLS), BF)] + [piece] * (4 * CHUNKS),
        in_specs=[smem(), vmem(), vmem(), vmem()],
        out_specs=[vmem()] * (1 + 4 * CHUNKS),
        compiler_params=params(8),
        cost_estimate=cost(0, 2_600_000),
        name="split_inputs",
    )(where, x, k, v)
    return out[0], [out[1 + CHUNKS * i : 1 + CHUNKS * (i + 1)] for i in range(4)]


def cast_kernel(where, ko, vo, kx, vx, own, other):
    own[:, :COLS] = ko[0].astype(BF)
    own[:, COLS:] = vo[0].astype(BF)
    other[:, :COLS] = kx[0].astype(BF)
    other[:, COLS:] = vx[0].astype(BF)


def cast_weights(where, kw, vw):
    n = QUARTER // TILE
    mine = pl.BlockSpec((1, TILE, COLS), lambda i, w: (0, w[2] * n + i, 0))
    theirs = pl.BlockSpec((1, TILE, COLS), lambda i, w: (0, (1 - w[2]) * n + i, 0))
    out = pl.BlockSpec((TILE, 2 * COLS), lambda i, w: (i, 0))
    shape = sds((QUARTER, 2 * COLS), BF)
    return pl.pallas_call(
        cast_kernel,
        out_shape=[shape, shape],
        grid_spec=pltpu.PrefetchScalarGridSpec(
            num_scalar_prefetch=1,
            grid=(n,),
            in_specs=[mine, mine, theirs, theirs],
            out_specs=[out, out],
        ),
        compiler_params=params(8),
        cost_estimate=cost(0, 6 * MB),
        name="cast_weights",
    )(where, kw, vw, kw, vw)


def order_kernel(where, own, core, other, othercore, out):
    y, c = where[1], where[2]
    for j in range(4):
        for cr in range(2):
            chip = lax.rem(y + j, 4)
            row = pl.multiple_of(chip * 2 * ROWS + (c + cr - 2 * c * cr) * ROWS, ROWS)
            to = j * 256 + cr * ROWS
            out[to : to + ROWS, : 2 * COLS] = own[pl.ds(row, ROWS), :]
            out[to : to + ROWS, 2 * COLS :] = core[pl.ds(row, ROWS), :]
            to += 128
            out[to : to + ROWS, : 2 * COLS] = other[pl.ds(row, ROWS), :]
            out[to : to + ROWS, 2 * COLS :] = othercore[pl.ds(row, ROWS), :]


def order_cotangents(where, own, core, other, othercore):
    return pl.pallas_call(
        order_kernel,
        out_shape=sds((1024, 512), BF),
        in_specs=[smem()] + [vmem()] * 4,
        out_specs=vmem(),
        compiler_params=params(8),
        cost_estimate=cost(0, 2 * MB),
        name="order_cotangents",
    )(where, own, core, other, othercore)


NT = (((1,), (1,)), ((), ()))
TN = (((0,), (0,)), ((), ()))
DXT = 512


def dx_kernel(kv, w0, w1, *outs):
    part = lax.dot_general(kv[:, :256], w0[...], NT, preferred_element_type=F32)
    part += lax.dot_general(kv[:, 256:], w1[...], NT, preferred_element_type=F32)
    part = (part * SCALING).astype(BF)
    for g in range(2):
        base = 128 * (1 - g)
        oa, ob, right, left, own = outs[5 * g : 5 * g + 5]
        oa[...] = part[512 + base : 512 + base + 64]
        ob[...] = part[512 + base + 64 : 512 + base + 128]
        right[...] = part[256 + base : 256 + base + 128]
        left[...] = part[768 + base : 768 + base + 128]
        own[...] = part[base : base + 128]


def input_terms(kv, w0, w1):
    small, large = sds((64, QUARTER), BF), sds((128, QUARTER), BF)
    sspec = pl.BlockSpec((64, DXT), lambda i: (0, i))
    lspec = pl.BlockSpec((128, DXT), lambda i: (0, i))
    wspec = pl.BlockSpec((DXT, 256), lambda i: (i, 0))
    return pl.pallas_call(
        dx_kernel,
        out_shape=[small, small, large, large, large] * 2,
        grid=(QUARTER // DXT,),
        in_specs=[pl.BlockSpec((1024, 512), lambda i: (0, 0)), wspec, wspec],
        out_specs=[sspec, sspec, lspec, lspec, lspec] * 2,
        compiler_params=params(16),
        cost_estimate=cost(2 * 1024 * 512 * QUARTER, 7 * MB),
        name="input_terms",
    )(kv, w0, w1)


def dw_kernel(kv, *refs):
    xs, (own, send) = refs[:8], refs[8:]
    x = jnp.concatenate([r[...] for r in xs], axis=0)
    g = lax.dot_general(x, kv[...], TN, preferred_element_type=F32) * SCALING
    own[...] = g[:, :256]
    send[...] = g[:, 256:].astype(BF)


def weight_terms(kv, xs):
    t = 256
    return pl.pallas_call(
        dw_kernel,
        out_shape=[sds((CH, 256), F32), sds((CH, 256), BF)],
        grid=(CH // t,),
        in_specs=[pl.BlockSpec((1024, 512), lambda i: (0, 0))]
        + [pl.BlockSpec((128, t), lambda i: (0, i))] * 8,
        out_specs=[pl.BlockSpec((t, 256), lambda i: (i, 0))] * 2,
        compiler_params=params(16),
        cost_estimate=cost(2 * 1024 * 512 * CH, 5 * MB),
        name="weight_terms",
    )(kv, *xs)


def proj_kernel(*refs):
    xs, (w0, w1), (own, send), acc = refs[:8], refs[8:10], refs[10:12], refs[12]
    i = pl.program_id(0)
    w = jnp.concatenate([w0[...], w1[...]], axis=1)
    x = jnp.concatenate([r[...] for r in xs], axis=0)
    part = jnp.dot(x, w, preferred_element_type=F32) * SCALING

    @pl.when(i == 0)
    def _():
        acc[...] = part

    @pl.when(i > 0)
    def _():
        acc[...] += part

    @pl.when(i == pl.num_programs(0) - 1)
    def _():
        own[...] = acc[:, :256]
        send[...] = acc[:, 256:].astype(BF)


def projection(chunk, prev, xs, w0, w1):
    t = 512
    n = CH // t
    wspec = pl.BlockSpec((t, 256), lambda i: (chunk * n + i, 0))
    return pl.pallas_call(
        proj_kernel,
        out_shape=[sds((1024, 256), F32), sds((1024, 256), BF)],
        grid=(n,),
        in_specs=[pl.BlockSpec((128, t), lambda i: (0, i))] * 8 + [wspec] * 2,
        out_specs=[pl.BlockSpec((1024, 256), lambda i: (0, 0))] * 2,
        scratch_shapes=[pltpu.VMEM((1024, 512), F32)],
        compiler_params=params(16),
        cost_estimate=cost(2 * 1024 * 512 * CH, 5 * MB),
        name="projection",
    )(*xs, w0, w1)


def proj_sum_kernel(a, b, ra, rb, keep, send):
    for at in range(0, 1024, 64):
        j, o, cr = at // 256, at // 128 % 2, at // 64 % 2
        far = at + 64 - 128 * cr
        total = (
            a[at : at + 64] + b[at : at + 64] + ra[far : far + 64].astype(F32) + rb[far : far + 64].astype(F32)
        )
        to = j * 128 + cr * 64
        if o:
            send[to : to + 64] = total.astype(BF)
        else:
            keep[to : to + 64] = total


def projection_sum(a, b, ra, rb):
    return pl.pallas_call(
        proj_sum_kernel,
        out_shape=[sds((512, 256), F32), sds((512, 256), BF)],
        in_specs=[vmem()] * 4,
        out_specs=[vmem()] * 2,
        compiler_params=params(8),
        cost_estimate=cost(0, 4 * MB),
        name="projection_sum",
    )(a, b, ra, rb)


def proj_end_kernel(where, keep, got, keys, values):
    y, c = where[1], where[2]
    for j in range(4):
        for cr in range(2):
            chip = lax.rem(y + j, 4)
            row = pl.multiple_of(chip * 2 * ROWS + (c + cr - 2 * c * cr) * ROWS, ROWS)
            at = j * 128 + cr * ROWS
            total = (keep[at : at + ROWS] + got[at : at + ROWS].astype(F32)).astype(BF)
            keys[pl.ds(row, ROWS), :] = total[:, :COLS]
            values[pl.ds(row, ROWS), :] = total[:, COLS:]


def projection_end(where, keep, got):
    out = sds((512, COLS), BF)
    return pl.pallas_call(
        proj_end_kernel,
        out_shape=[out, out],
        in_specs=[smem()] + [vmem()] * 2,
        out_specs=[vmem()] * 2,
        compiler_params=params(8),
        cost_estimate=cost(0, MB),
        name="projection_end",
    )(where, keep, got)


def sum3_kernel(a, b, c, lo, hi):
    total = (a[...].astype(F32) + b[...].astype(F32) + c[...].astype(F32)).astype(BF)
    lo[...] = total[:64]
    hi[...] = total[64:]


def sum3(a, b, c):
    out = sds((64, QUARTER), BF)
    return pl.pallas_call(
        sum3_kernel,
        out_shape=[out, out],
        in_specs=[vmem()] * 3,
        out_specs=[vmem()] * 2,
        compiler_params=params(8),
        cost_estimate=cost(0, 2 * MB),
        name="sum_terms",
    )(a, b, c)


def join_kernel(where, own, core, z, zc, out):
    f, c = where[0], where[2]
    quarters = (2 * f + c, 2 * f + 1 - c, 2 * (1 - f) + c, 2 * (1 - f) + 1 - c)
    for q, ref in zip(quarters, (own, core, z, zc)):
        out[:, pl.ds(pl.multiple_of(q * QUARTER, QUARTER), QUARTER)] = ref[...]


def join(where, own, core, z, zc):
    return pl.pallas_call(
        join_kernel,
        out_shape=sds((ROWS, D), BF),
        in_specs=[smem()] + [vmem()] * 4,
        out_specs=vmem(),
        compiler_params=params(8),
        cost_estimate=cost(0, 2 * MB),
        name="join_input_grad",
    )(where, own, core, z, zc)


def chunk_specs(chunk):
    n = CH // TILE
    per_quarter = QUARTER // TILE

    def at(s, i, w):
        q = s + w[2] - 2 * s * w[2]
        return (0, q * per_quarter + chunk * n + i, 0)

    whole = pl.BlockSpec((1, TILE, COLS), at)
    term = pl.BlockSpec((TILE, 256), lambda s, i, w: (i, 0))
    moved = pl.BlockSpec((TILE, 256), lambda s, i, w: (s * n + i, 0))
    return (2, n), whole, term, moved


def step_kernel(where, kw, vw, km, vm, own, got, *refs):
    nkm, nvm, moved = refs[-3:]
    s = pl.program_id(0)

    def run(g):
        k = momentum_decay * km[0] + g[:, :COLS]
        v = momentum_decay * vm[0] + g[:, COLS:]
        nkm[0] = k
        nvm[0] = v
        moved[:, :COLS] = (kw[0] - learn_rate * k).astype(BF)
        moved[:, COLS:] = (vw[0] - learn_rate * v).astype(BF)

    @pl.when(s == 0)
    def _():
        run(own[...])

    @pl.when(s == 1)
    def _():
        run(got[...].astype(F32))


def step(where, chunk, kw, vw, km, vm, own, got, before):
    grid, whole, term, moved = chunk_specs(chunk)
    full = sds((1, HALF, COLS), F32)
    extra = [] if before is None else list(before)
    anyspec = pl.BlockSpec(memory_space=pl.ANY)
    return pl.pallas_call(
        step_kernel,
        out_shape=[full, full, sds((2 * CH, 256), BF)],
        grid_spec=pltpu.PrefetchScalarGridSpec(
            num_scalar_prefetch=1,
            grid=grid,
            in_specs=[whole] * 4 + [term] * 2 + [anyspec] * len(extra),
            out_specs=[whole, whole, moved],
        ),
        input_output_aliases={7: 0, 8: 1} if extra else {},
        compiler_params=params(16),
        cost_estimate=cost(0, 8 * MB),
        name="momentum_step",
    )(where, kw, vw, km, vm, own, got, *extra)


def mean_kernel(where, kw, vw, nkm, nvm, got, *refs):
    nkw, nvw = refs[-2:]
    nkw[0] = 0.5 * ((kw[0] - learn_rate * nkm[0]) + got[:, :COLS].astype(F32))
    nvw[0] = 0.5 * ((vw[0] - learn_rate * nvm[0]) + got[:, COLS:].astype(F32))


def mean(where, chunk, kw, vw, nkm, nvm, got, before):
    grid, whole, term, moved = chunk_specs(chunk)
    full = sds((1, HALF, COLS), F32)
    extra = [] if before is None else list(before)
    anyspec = pl.BlockSpec(memory_space=pl.ANY)
    return pl.pallas_call(
        mean_kernel,
        out_shape=[full, full],
        grid_spec=pltpu.PrefetchScalarGridSpec(
            num_scalar_prefetch=1,
            grid=grid,
            in_specs=[whole] * 4 + [moved] + [anyspec] * len(extra),
            out_specs=[whole, whole],
        ),
        input_output_aliases={6: 0, 7: 1} if extra else {},
        compiler_params=params(16),
        cost_estimate=cost(0, 8 * MB),
        name="average",
    )(where, kw, vw, nkm, nvm, got, *extra)


def to_right(a):
    return lax.ppermute(a, "tensor", [(t, (t + 2) % 8) for t in range(8)])


def to_left(a):
    return lax.ppermute(a, "tensor", [(t, (t + 6) % 8) for t in range(8)])


def to_core(a):
    return lax.ppermute(a, "tensor", [(t, t ^ 1) for t in range(8)])


def to_z(a):
    return lax.ppermute(a, "fsdp", [(0, 1), (1, 0)])


def to_z_core(a):
    return lax.ppermute(a, ("fsdp", "tensor"), [(i, i ^ 9) for i in range(16)])


def to_partner(a, bit):
    n = lax.axis_size("gossip")
    return lax.ppermute(a, "gossip", [(i, i ^ (1 << bit)) for i in range(n)])


def whole_step(bit, where, normed, kc, vc, kw, vw, km, vm):
    kv_own, (x_own, x_core, x_z, x_zc) = split_inputs(where, normed, kc, vc)
    kv_z = to_z(kv_own)
    gathered = []
    for h in range(CHUNKS):
        a0 = jnp.concatenate([x_own[h], to_core(x_core[h])], axis=0)
        a3, a1 = to_right(a0), to_left(a0)
        b0 = jnp.concatenate([to_z(x_z[h]), to_z_core(x_zc[h])], axis=0)
        b3, b1 = to_right(b0), to_left(b0)
        a2, b2 = to_right(a3), to_left(b1)
        gathered.append([a0, b0, a1, b1, a2, b2, a3, b3])
    w_own, w_send = cast_weights(where, kw, vw)
    w_core = to_core(w_send)
    kv = order_cotangents(where, kv_own, to_core(kv_own), kv_z, to_core(kv_z))

    momenta, moved, weights = None, [], None
    for h in range(CHUNKS):
        own, send = weight_terms(kv, gathered[h])
        *momenta, m = step(where, h, kw, vw, km, vm, own, to_core(send), momenta)
        moved.append(m)
    got = [to_partner(m, bit) for m in moved]

    terms = input_terms(kv, w_own, w_core)
    ends = []
    for g in range(2):
        oa, ob, right, left, mine = terms[5 * g : 5 * g + 5]
        ra, rb = to_right(oa), to_left(ob)
        right = jnp.concatenate([right[:64] + ra, right[64:]], axis=0)
        left = jnp.concatenate([left[:64], left[64:] + rb], axis=0)
        ends.append(sum3(mine, to_right(right), to_left(left)))
    (o_z, o_zc), (s_own, s_core) = ends
    input_grad = join(where, s_own, to_core(s_core), to_z(o_z), to_z_core(o_zc))

    pa, sa = projection(0, None, gathered[0], w_own, w_core)
    pb, sb = projection(1, None, gathered[1], w_own, w_core)
    keep, send = projection_sum(pa, pb, to_core(sa), to_core(sb))
    keys, values = projection_end(where, keep, to_z(send))

    for h in range(CHUNKS):
        weights = mean(where, h, kw, vw, *momenta, got[h], weights)
    return keys, values, input_grad, *weights, *momenta


def per_device(normed, kc, vc, kw, vw, km, vm, step_index):
    t = lax.axis_index("tensor")
    where = jnp.stack([lax.axis_index("fsdp"), t // 2, t % 2]).astype(jnp.int32)
    levels = lax.axis_size("gossip").bit_length() - 1
    branches = [partial(whole_step, bit) for bit in range(levels)]
    return lax.switch(step_index % levels, branches, where, normed, kc, vc, kw, vw, km, vm)


def solution(mesh):
    rows = P(("gossip", "fsdp", "tensor"), None)
    heads = P(("gossip", "fsdp"), "tensor")
    weight = P("gossip", "fsdp", "tensor")
    return jax.shard_map(
        per_device,
        mesh=mesh,
        in_specs=(rows, heads, heads, weight, weight, weight, weight, P()),
        out_specs=(heads, heads, rows, weight, weight, weight, weight),
        check_vma=False,
    )
```

```python
from functools import partial

import jax
import jax.numpy as jnp
from jax import lax
from jax.experimental import pallas as pl
from jax.experimental.pallas import tpu as pltpu
from jax.sharding import PartitionSpec as P

D = 8192
SCALING = D ** (-0.5)
momentum_decay = 0.9
learn_rate = 0.5

F32 = jnp.float32
BF = jnp.bfloat16
HALF = 4096
QUARTER = 2048
CHUNKS = 2
CH = QUARTER // CHUNKS
ROWS = 64
TOK = 512
COLS = 128
TILE = 512

MB = 1024 * 1024


def sds(shape, dtype):
    return jax.ShapeDtypeStruct(shape, dtype)


def params(mib):
    return pltpu.CompilerParams(vmem_limit_bytes=mib * MB)


def cost(flops, nbytes):
    return pl.CostEstimate(flops=flops // 1000, bytes_accessed=nbytes // 1000, transcendentals=0)


def in_hbm(x):
    return pltpu.with_memory_space_constraint(x, pltpu.HBM)


def smem():
    return pl.BlockSpec(memory_space=pltpu.SMEM)


def vmem():
    return pl.BlockSpec(memory_space=pltpu.VMEM)


def copies(pairs, sems):
    started = [pltpu.make_async_copy(src, dst, sems.at[i]) for i, (src, dst) in enumerate(pairs)]
    for copy in started:
        copy.start()
    for copy in started:
        copy.wait()


def anywhere():
    return pl.BlockSpec(memory_space=pl.ANY)


def split_kernel(where, x, k, v, kv, core, own, other, sems):
    f, c = where[0], where[2]
    pairs = []
    for g, out in enumerate((own, other)):
        q = 2 * (f + g - 2 * f * g)
        start = pl.multiple_of((q + 1 - c) * QUARTER, QUARTER)
        pairs.append((x.at[:, pl.ds(start, QUARTER)], core.at[:, g * QUARTER : (g + 1) * QUARTER]))
        start = pl.multiple_of((q + c) * QUARTER, QUARTER)
        pairs.append((x.at[:, pl.ds(start, QUARTER)], out))
    pairs += [(k, kv.at[:, :COLS]), (v, kv.at[:, COLS:])]
    copies(pairs, sems)


def split_inputs(where, x, k, v):
    piece = sds((ROWS, QUARTER), BF)
    return pl.pallas_call(
        split_kernel,
        out_shape=[sds((TOK, 2 * COLS), BF), sds((ROWS, 2 * QUARTER), BF), piece, piece],
        in_specs=[smem()] + [anywhere()] * 3,
        out_specs=[anywhere()] * 4,
        scratch_shapes=[pltpu.SemaphoreType.DMA((6,))],
        compiler_params=params(4),
        cost_estimate=cost(0, 2_600_000),
        name="split_inputs",
    )(where, x, k, v)


def cast_kernel(where, ko, vo, kx, vx, own, other):
    own[:, :COLS] = ko[0].astype(BF)
    own[:, COLS:] = vo[0].astype(BF)
    other[:, :COLS] = kx[0].astype(BF)
    other[:, COLS:] = vx[0].astype(BF)


def cast_weights(where, kw, vw):
    n = QUARTER // TILE
    mine = pl.BlockSpec((1, TILE, COLS), lambda i, w: (0, w[2] * n + i, 0))
    theirs = pl.BlockSpec((1, TILE, COLS), lambda i, w: (0, (1 - w[2]) * n + i, 0))
    out = pl.BlockSpec((TILE, 2 * COLS), lambda i, w: (i, 0))
    shape = sds((QUARTER, 2 * COLS), BF)
    return pl.pallas_call(
        cast_kernel,
        out_shape=[shape, shape],
        grid_spec=pltpu.PrefetchScalarGridSpec(
            num_scalar_prefetch=1,
            grid=(n,),
            in_specs=[mine, mine, theirs, theirs],
            out_specs=[out, out],
        ),
        compiler_params=params(8),
        cost_estimate=cost(0, 6 * MB),
        name="cast_weights",
    )(where, kw, vw, kw, vw)


def pre_kernel(where, kw, vw, km, vm, *pre):
    h = pl.program_id(0)
    for chunk in range(CHUNKS):

        @pl.when(h == chunk)
        def _():
            pre[chunk][:, :COLS] = kw[0] - (learn_rate * momentum_decay) * km[0]
            pre[chunk][:, COLS:] = vw[0] - (learn_rate * momentum_decay) * vm[0]


def moved_by_old(where, kw, vw, km, vm):
    n = CH // TILE

    def at(h, s, i, w):
        q = s + w[2] - 2 * s * w[2]
        return (0, (q * CHUNKS + h) * n + i, 0)

    def chunk_at(chunk):
        def index(h, s, i, w):
            inside = s * n + i
            return (jnp.where(h == chunk, inside, jnp.where(h < chunk, 0, 2 * n - 1)), 0)

        return index

    whole = pl.BlockSpec((1, TILE, COLS), at)
    return pl.pallas_call(
        pre_kernel,
        out_shape=[sds((2 * CH, 256), F32)] * CHUNKS,
        grid_spec=pltpu.PrefetchScalarGridSpec(
            num_scalar_prefetch=1,
            grid=(CHUNKS, 2, n),
            in_specs=[whole] * 4,
            out_specs=[pl.BlockSpec((TILE, 256), chunk_at(chunk)) for chunk in range(CHUNKS)],
        ),
        compiler_params=params(16),
        cost_estimate=cost(0, 12 * MB),
        name="moved_by_old_momentum",
    )(where, kw, vw, km, vm)


def order_kernel(where, own, core, out):
    y, c = where[1], where[2]
    for j in range(4):
        for cr in range(2):
            t = 2 * lax.rem(y + j, 4) + (c + cr - 2 * c * cr)
            for g in range(2):
                row = pl.multiple_of(t * 2 * ROWS + g * ROWS, ROWS)
                to = j * 256 + g * 128 + cr * ROWS
                out[to : to + ROWS, : 2 * COLS] = own[pl.ds(row, ROWS), :]
                out[to : to + ROWS, 2 * COLS :] = core[pl.ds(row, ROWS), :]


def order_cotangents(where, own, core):
    return pl.pallas_call(
        order_kernel,
        out_shape=sds((1024, 512), BF),
        in_specs=[smem()] + [vmem()] * 2,
        out_specs=vmem(),
        compiler_params=params(8),
        cost_estimate=cost(0, 2 * MB),
        name="order_cotangents",
    )(where, own, core)


NT = (((1,), (1,)), ((), ()))
TN = (((0,), (0,)), ((), ()))
DXT = 512


def dx_kernel(kv, w0, w1, *outs):
    part = lax.dot_general(kv[:, :256], w0[...], NT, preferred_element_type=F32)
    part += lax.dot_general(kv[:, 256:], w1[...], NT, preferred_element_type=F32)
    part = (part * SCALING).astype(BF)
    for g in range(2):
        for out, chip in zip(outs[4 * g : 4 * g + 4], (2, 1, 3, 0)):
            base = 256 * chip + 128 * (1 - g)
            out[...] = part[base : base + 128]


def input_terms(kv, w0, w1):
    spec = pl.BlockSpec((128, DXT), lambda i: (0, i))
    wspec = pl.BlockSpec((DXT, 256), lambda i: (i, 0))
    return pl.pallas_call(
        dx_kernel,
        out_shape=[sds((128, QUARTER), BF)] * 8,
        grid=(QUARTER // DXT,),
        in_specs=[pl.BlockSpec((1024, 512), lambda i: (0, 0)), wspec, wspec],
        out_specs=[spec] * 8,
        compiler_params=params(16),
        cost_estimate=cost(2 * 1024 * 512 * QUARTER, 7 * MB),
        name="input_terms",
    )(kv, w0, w1)


def dw_kernel(kv, *refs):
    xs, (own, send) = refs[:8], refs[8:]
    x = jnp.concatenate([r[...] for r in xs], axis=0)
    g = lax.dot_general(x, kv[...], TN, preferred_element_type=F32) * SCALING
    own[...] = g[:, :256]
    send[...] = g[:, 256:].astype(BF)


def weight_terms(chunk, kv, xs):
    t = 256
    n = CH // t
    return pl.pallas_call(
        dw_kernel,
        out_shape=[sds((CH, 256), F32), sds((CH, 256), BF)],
        grid=(n,),
        in_specs=[pl.BlockSpec((1024, 512), lambda i: (0, 0))]
        + [pl.BlockSpec((128, t), lambda i: (0, chunk * n + i))] * 8,
        out_specs=[pl.BlockSpec((t, 256), lambda i: (i, 0))] * 2,
        compiler_params=params(16),
        cost_estimate=cost(2 * 1024 * 512 * CH, 5 * MB),
        name="weight_terms",
    )(kv, *xs)


def proj_kernel(*refs):
    xs, (w0, w1), (own, send), acc = refs[:8], refs[8:10], refs[10:12], refs[12]
    i = pl.program_id(0)
    w = jnp.concatenate([w0[...], w1[...]], axis=1)

    @pl.when(i == 0)
    def _():
        acc[...] = jnp.zeros_like(acc)

    for k in range(8):
        rows = slice(128 * k, 128 * k + 128)
        acc[rows] += jnp.dot(xs[k][...], w, preferred_element_type=F32)

    @pl.when(i == pl.num_programs(0) - 1)
    def _():
        own[...] = acc[:, :256] * SCALING
        send[...] = (acc[:, 256:] * SCALING).astype(BF)


def projection(*args):
    t = 512
    wspec = pl.BlockSpec((t, 256), lambda i: (i, 0))
    return pl.pallas_call(
        proj_kernel,
        out_shape=[sds((1024, 256), F32), sds((1024, 256), BF)],
        grid=(QUARTER // t,),
        in_specs=[pl.BlockSpec((128, t), lambda i: (0, i))] * 8 + [wspec] * 2,
        out_specs=[pl.BlockSpec((1024, 256), lambda i: (0, 0))] * 2,
        scratch_shapes=[pltpu.VMEM((1024, 512), F32)],
        compiler_params=params(16),
        cost_estimate=cost(2 * 1024 * 512 * QUARTER, 8 * MB),
        name="projection",
    )(*args)


def proj_sum_kernel(own, got, keep, send):
    for at in range(0, 1024, 64):
        j, o, cr = at // 256, at // 128 % 2, at // 64 % 2
        far = at + 64 - 128 * cr
        total = own[at : at + 64] + got[far : far + 64].astype(F32)
        to = j * 128 + cr * 64
        if o:
            send[to : to + 64] = total.astype(BF)
        else:
            keep[to : to + 64] = total


def projection_sum(own, got):
    return pl.pallas_call(
        proj_sum_kernel,
        out_shape=[sds((512, 256), F32), sds((512, 256), BF)],
        in_specs=[vmem()] * 2,
        out_specs=[vmem()] * 2,
        compiler_params=params(8),
        cost_estimate=cost(0, 2 * MB),
        name="projection_sum",
    )(own, got)


def proj_end_kernel(where, keep, got, keys, values):
    y, c = where[1], where[2]
    for j in range(4):
        for cr in range(2):
            chip = lax.rem(y + j, 4)
            row = pl.multiple_of(chip * 2 * ROWS + (c + cr - 2 * c * cr) * ROWS, ROWS)
            at = j * 128 + cr * ROWS
            total = (keep[at : at + ROWS] + got[at : at + ROWS].astype(F32)).astype(BF)
            keys[pl.ds(row, ROWS), :] = total[:, :COLS]
            values[pl.ds(row, ROWS), :] = total[:, COLS:]


def projection_end(where, keep, got):
    out = pltpu.HBM((512, COLS), BF)
    return pl.pallas_call(
        proj_end_kernel,
        out_shape=[out, out],
        in_specs=[smem()] + [vmem()] * 2,
        out_specs=[vmem()] * 2,
        compiler_params=params(8),
        cost_estimate=cost(0, MB),
        name="projection_end",
    )(where, keep, got)


def sum3_kernel(a, b, c, lo, hi):
    total = (a[...].astype(F32) + b[...].astype(F32) + c[...].astype(F32)).astype(BF)
    lo[...] = total[:64]
    hi[...] = total[64:]


def sum3(a, b, c):
    out = sds((64, QUARTER), BF)
    return pl.pallas_call(
        sum3_kernel,
        out_shape=[out, out],
        in_specs=[vmem()] * 3,
        out_specs=[vmem()] * 2,
        compiler_params=params(8),
        cost_estimate=cost(0, 2 * MB),
        name="sum_terms",
    )(a, b, c)


def join_kernel(where, own, core, z, zc, out):
    f, c = where[0], where[2]
    quarters = (2 * f + c, 2 * f + 1 - c, 2 * (1 - f) + c, 2 * (1 - f) + 1 - c)
    for q, ref in zip(quarters, (own, core, z, zc)):
        out[:, pl.ds(pl.multiple_of(q * QUARTER, QUARTER), QUARTER)] = ref[...]


def join(where, own, core, z, zc):
    return pl.pallas_call(
        join_kernel,
        out_shape=pltpu.HBM((ROWS, D), BF),
        in_specs=[smem()] + [vmem()] * 4,
        out_specs=vmem(),
        compiler_params=params(8),
        cost_estimate=cost(0, 2 * MB),
        name="join_input_grad",
    )(where, own, core, z, zc)


def chunk_specs(chunk):
    n = CH // TILE
    per_quarter = QUARTER // TILE

    def at(s, i, w):
        q = s + w[2] - 2 * s * w[2]
        return (0, q * per_quarter + chunk * n + i, 0)

    whole = pl.BlockSpec((1, TILE, COLS), at)
    term = pl.BlockSpec((TILE, 256), lambda s, i, w: (i, 0))
    moved = pl.BlockSpec((TILE, 256), lambda s, i, w: (s * n + i, 0))
    return (2, n), whole, term, moved


def moved_kernel(pre, own, got, moved):
    moved[:CH] = (pre[:CH] - learn_rate * own[...]).astype(BF)
    moved[CH:] = (pre[CH:] - learn_rate * got[...].astype(F32)).astype(BF)


def moved_chunk(pre, own, got):
    return pl.pallas_call(
        moved_kernel,
        out_shape=sds((2 * CH, 256), BF),
        in_specs=[vmem()] * 3,
        out_specs=vmem(),
        compiler_params=params(8),
        cost_estimate=cost(0, 5 * MB),
        name="moved_weights",
    )(pre, own, got)


def momentum_kernel(where, km, vm, *refs):
    own, got, (nkm, nvm) = refs[:CHUNKS], refs[CHUNKS : 2 * CHUNKS], refs[2 * CHUNKS :]
    s, h = pl.program_id(0), pl.program_id(1)

    def run(g):
        nkm[0] = momentum_decay * km[0] + g[:, :COLS]
        nvm[0] = momentum_decay * vm[0] + g[:, COLS:]

    for chunk in range(CHUNKS):

        @pl.when((s == 0) & (h == chunk))
        def _():
            run(own[chunk][...])

        @pl.when((s == 1) & (h == chunk))
        def _():
            run(got[chunk][...].astype(F32))


def momentum_step(where, km, vm, own, got):
    n = CH // TILE

    def at(s, h, i, w):
        q = s + w[2] - 2 * s * w[2]
        return (0, (q * CHUNKS + h) * n + i, 0)

    whole = pl.BlockSpec((1, TILE, COLS), at)
    terms = [
        pl.BlockSpec(
            (TILE, 256),
            lambda s, h, i, w, kind=kind, chunk=chunk: (jnp.where((s == kind) & (h == chunk), i, 0), 0),
        )
        for kind in range(2)
        for chunk in range(CHUNKS)
    ]
    full = pltpu.HBM((1, HALF, COLS), F32)
    return pl.pallas_call(
        momentum_kernel,
        out_shape=[full, full],
        grid_spec=pltpu.PrefetchScalarGridSpec(
            num_scalar_prefetch=1,
            grid=(2, CHUNKS, n),
            in_specs=[whole] * 2 + terms,
            out_specs=[whole, whole],
        ),
        compiler_params=params(16),
        cost_estimate=cost(0, 11 * MB),
        name="momentum_step",
    )(where, km, vm, *own, *got)


def mean_kernel(where, pre, own, got, partner, *refs):
    nkw, nvw = refs[-2:]
    s = pl.program_id(0)

    def run(g):
        mean = 0.5 * ((pre[...] - learn_rate * g) + partner[...].astype(F32))
        nkw[0] = mean[:, :COLS]
        nvw[0] = mean[:, COLS:]

    @pl.when(s == 0)
    def _():
        run(own[...])

    @pl.when(s == 1)
    def _():
        run(got[...].astype(F32))


def mean(where, chunk, pre, own, got, partner, before):
    grid, whole, term, moved = chunk_specs(chunk)
    full = pltpu.HBM((1, HALF, COLS), F32)
    extra = [] if before is None else list(before)
    return pl.pallas_call(
        mean_kernel,
        out_shape=[full, full],
        grid_spec=pltpu.PrefetchScalarGridSpec(
            num_scalar_prefetch=1,
            grid=grid,
            in_specs=[moved, term, term, moved] + [anywhere()] * len(extra),
            out_specs=[whole, whole],
        ),
        input_output_aliases={5: 0, 6: 1} if extra else {},
        compiler_params=params(16),
        cost_estimate=cost(0, 8 * MB),
        name="average",
    )(where, pre, own, got, partner, *extra)


def to_right(a):
    return lax.ppermute(a, "tensor", [(t, (t + 2) % 8) for t in range(8)])


def to_left(a):
    return lax.ppermute(a, "tensor", [(t, (t + 6) % 8) for t in range(8)])


def to_core(a):
    return lax.ppermute(a, "tensor", [(t, t ^ 1) for t in range(8)])


def to_z(a):
    return lax.ppermute(a, "fsdp", [(0, 1), (1, 0)])


def to_z_core(a):
    return lax.ppermute(a, ("fsdp", "tensor"), [(i, i ^ 9) for i in range(16)])


def to_partner(a, bit):
    n = lax.axis_size("gossip")
    return lax.ppermute(a, "gossip", [(i, i ^ (1 << bit)) for i in range(n)])


def after(value, *others):
    return lax.optimization_barrier((value, others))[0]


def exchange(bit, where, km, vm, kv, pre, terms, xs, w_own, w_core):
    own, send = weight_terms(0, kv, xs)
    got = to_core(send)
    partner = to_partner(moved_chunk(pre[0], own, got), bit)
    o_terms, s_terms = terms[:4], terms[4:]
    o_left = to_left(o_terms[2])
    o_relayed = o_terms[1] + to_right(o_terms[0])
    own1, send = weight_terms(1, after(kv, own), xs)
    got1 = to_core(send)
    partner1 = to_partner(after(moved_chunk(pre[1], own1, got1), partner), bit)
    p_own, p_send = projection(*xs, w_own, w_core)
    o_right = to_right(after(o_relayed, p_send))
    keep, p_send = projection_sum(p_own, to_core(p_send))
    keys, values = projection_end(where, keep, to_z(p_send))
    o_z, o_zc = sum3(o_terms[3], o_right, o_left)
    z, zc = to_z(o_z), to_z_core(o_zc)
    s_left = to_left(s_terms[2] + to_left(after(s_terms[0], o_left)))
    s_right = to_right(after(s_terms[1], o_right))
    momenta = momentum_step(after(where, o_z), km, vm, (own, own1), (got, got1))
    weights = mean(where, 0, pre[0], own, got, partner, None)
    s_own, s_core = sum3(after(s_terms[3], momenta, weights), s_right, s_left)
    input_grad = join(where, s_own, to_core(s_core), z, zc)
    weights = mean(where, 1, pre[1], own1, got1, partner1, weights)
    return keys, values, input_grad, *weights, *momenta


def per_device(normed, kc, vc, kw, vw, km, vm, step_index):
    t = lax.axis_index("tensor")
    where = jnp.stack([lax.axis_index("fsdp"), t // 2, t % 2]).astype(jnp.int32)
    levels = lax.axis_size("gossip").bit_length() - 1
    bit = step_index % levels

    normed, kc, vc, kw, vw, km, vm = map(in_hbm, (normed, kc, vc, kw, vw, km, vm))
    kv_own, x_core, x_own, x_z = split_inputs(where, normed, kc, vc)
    kv_z = to_z(kv_own)
    x_core = to_core(x_core)
    a = jnp.concatenate([x_own, x_core[:, :QUARTER]], axis=0)
    b = to_z(jnp.concatenate([x_z, x_core[:, QUARTER:]], axis=0))
    a3, a1 = to_right(a), to_left(a)
    pre = moved_by_old(after(where, a), kw, vw, km, vm)
    kv = jnp.stack([kv_own.reshape(8, ROWS, 256), kv_z.reshape(8, ROWS, 256)], axis=1).reshape(1024, 256)
    kv = order_cotangents(where, kv, to_core(kv))
    a2 = to_right(after(a3, pre[0]))
    b = after(b, a1, a3, pre[0])
    b3, b1 = to_right(b), to_left(b)
    w_own, w_send = cast_weights(after(where, b), kw, vw)
    b2 = to_left(after(b1, w_send))
    w_core = to_core(w_send)
    terms = input_terms(kv, w_own, w_core)
    xs = (a, b, a1, b1, a2, b2, a3, b3)
    kv = after(kv, terms[0])
    return lax.switch(
        bit,
        [partial(exchange, k) for k in range(levels)],
        where, km, vm, kv, pre, terms, xs, w_own, w_core,
    )


def solution(mesh):
    rows = P(("gossip", "fsdp", "tensor"), None)
    heads = P(("gossip", "fsdp"), "tensor")
    weight = P("gossip", "fsdp", "tensor")
    return jax.shard_map(
        per_device,
        mesh=mesh,
        in_specs=(rows, heads, heads, weight, weight, weight, weight, P()),
        out_specs=(heads, heads, rows, weight, weight, weight, weight),
        check_vma=False,
    )
```

```python
from functools import partial

import jax
import jax.numpy as jnp
from jax import lax
from jax.experimental import pallas as pl
from jax.experimental.pallas import tpu as pltpu
from jax.sharding import PartitionSpec as P

D = 8192
SCALING = D ** (-0.5)
momentum_decay = 0.9
learn_rate = 0.5

F32 = jnp.float32
BF = jnp.bfloat16
HALF = 4096
QUARTER = 2048
CHUNKS = 2
CH = QUARTER // CHUNKS
ROWS = 64
TOK = 512
COLS = 128
TILE = 1024

MB = 1024 * 1024


def sds(shape, dtype):
    return jax.ShapeDtypeStruct(shape, dtype)


def params(mib):
    return pltpu.CompilerParams(vmem_limit_bytes=mib * MB)


def cost(flops, nbytes):
    return pl.CostEstimate(flops=flops // 1000, bytes_accessed=nbytes // 1000, transcendentals=0)


def in_hbm(x):
    return pltpu.with_memory_space_constraint(x, pltpu.HBM)


def by_rows(rows, body, size=128):
    @pl.loop(0, rows // size)
    def _(i):
        body(pl.ds(pl.multiple_of(i * size, size), size))


def smem():
    return pl.BlockSpec(memory_space=pltpu.SMEM)


def vmem():
    return pl.BlockSpec(memory_space=pltpu.VMEM)


def copies(pairs, sems):
    started = [pltpu.make_async_copy(src, dst, sems.at[i]) for i, (src, dst) in enumerate(pairs)]
    for copy in started:
        copy.start()
    for copy in started:
        copy.wait()


def anywhere():
    return pl.BlockSpec(memory_space=pl.ANY)


def split_kernel(where, x, k, v, kv, core_own, core_other, own, other, sems):
    core = (core_own, core_other)
    f, c = where[0], where[2]
    pairs = []
    for g, out in enumerate((own, other)):
        q = 2 * (f + g - 2 * f * g)
        start = pl.multiple_of((q + 1 - c) * QUARTER, QUARTER)
        pairs.append((x.at[:, pl.ds(start, QUARTER)], core[g]))
        start = pl.multiple_of((q + c) * QUARTER, QUARTER)
        pairs.append((x.at[:, pl.ds(start, QUARTER)], out))
    pairs += [(k, kv.at[:, :COLS]), (v, kv.at[:, COLS:])]
    copies(pairs, sems)


def split_inputs(where, x, k, v):
    piece = sds((ROWS, QUARTER), BF)
    return pl.pallas_call(
        split_kernel,
        out_shape=[sds((TOK, 2 * COLS), BF), piece, piece, piece, piece],
        in_specs=[smem()] + [anywhere()] * 3,
        out_specs=[anywhere()] * 5,
        scratch_shapes=[pltpu.SemaphoreType.DMA((6,))],
        compiler_params=params(4),
        cost_estimate=cost(0, 2_600_000),
        name="split_inputs",
    )(where, x, k, v)


def prepare_kernel(where, kw, vw, km, vm, w_own, w_send, *pre):
    h, s = pl.program_id(0), pl.program_id(1)
    halves = ((kw, km, slice(0, COLS)), (vw, vm, slice(COLS, 2 * COLS)))
    for chunk in range(CHUNKS):
        for kind, rounded in ((0, w_own), (1, w_send)):

            @pl.when((h == chunk) & (s == kind))
            def _():
                def body(rows):
                    for w, m, cols in halves:
                        value = w[0, rows, :]
                        pre[chunk][rows, cols] = value - (learn_rate * momentum_decay) * m[0, rows, :]
                        rounded[rows, cols] = value.astype(BF)

                by_rows(TILE, body)


def prepare(where, kw, vw, km, vm):
    n = CH // TILE

    def at(h, s, i, w):
        q = s + w[2] - 2 * s * w[2]
        return (0, (q * CHUNKS + h) * n + i, 0)

    def chunk_at(chunk):
        def index(h, s, i, w):
            inside = s * n + i
            return (jnp.where(h == chunk, inside, jnp.where(h < chunk, 0, 2 * n - 1)), 0)

        return index

    whole = pl.BlockSpec((1, TILE, COLS), at)
    tile = (TILE, 256)
    return pl.pallas_call(
        prepare_kernel,
        out_shape=[sds((QUARTER, 256), BF)] * 2 + [sds((2 * CH, 256), F32)] * CHUNKS,
        grid_spec=pltpu.PrefetchScalarGridSpec(
            num_scalar_prefetch=1,
            grid=(CHUNKS, 2, n),
            in_specs=[whole] * 4,
            out_specs=[
                pl.BlockSpec(tile, lambda h, s, i, w: (h * n + jnp.where(s == 0, i, n - 1), 0)),
                pl.BlockSpec(tile, lambda h, s, i, w: (h * n + jnp.where(s == 1, i, 0), 0)),
            ]
            + [pl.BlockSpec(tile, chunk_at(chunk)) for chunk in range(CHUNKS)],
        ),
        compiler_params=params(24),
        cost_estimate=cost(0, 14 * MB),
        name="prepare_weights",
    )(where, kw, vw, km, vm)


def order_kernel(where, own, core, out):
    y, c = where[1], where[2]
    for j in range(4):
        for cr in range(2):
            t = 2 * lax.rem(y + j, 4) + (c + cr - 2 * c * cr)
            for g in range(2):
                row = pl.multiple_of(t * 2 * ROWS + g * ROWS, ROWS)
                to = j * 256 + g * 128 + cr * ROWS
                out[to : to + ROWS, : 2 * COLS] = own[pl.ds(row, ROWS), :]
                out[to : to + ROWS, 2 * COLS :] = core[pl.ds(row, ROWS), :]


def order_cotangents(where, own, core):
    return pl.pallas_call(
        order_kernel,
        out_shape=sds((1024, 512), BF),
        in_specs=[smem()] + [vmem()] * 2,
        out_specs=vmem(),
        compiler_params=params(8),
        cost_estimate=cost(0, 2 * MB),
        name="order_cotangents",
    )(where, own, core)


NT = (((1,), (1,)), ((), ()))
TN = (((0,), (0,)), ((), ()))
DXT = 1024


def dx_kernel(kv, w0, w1, *outs):
    part = lax.dot_general(kv[:, :256], w0[...], NT, preferred_element_type=F32)
    part += lax.dot_general(kv[:, 256:], w1[...], NT, preferred_element_type=F32)
    part = (part * SCALING).astype(BF)
    for g in range(2):
        for out, chip in zip(outs[4 * g : 4 * g + 4], (2, 1, 3, 0)):
            base = 256 * chip + 128 * (1 - g)
            out[...] = part[base : base + 128]


def input_terms(kv, w0, w1):
    spec = pl.BlockSpec((128, DXT), lambda i: (0, i))
    wspec = pl.BlockSpec((DXT, 256), lambda i: (i, 0))
    return pl.pallas_call(
        dx_kernel,
        out_shape=[sds((128, QUARTER), BF)] * 8,
        grid=(QUARTER // DXT,),
        in_specs=[pl.BlockSpec((1024, 512), lambda i: (0, 0)), wspec, wspec],
        out_specs=[spec] * 8,
        compiler_params=params(24),
        cost_estimate=cost(2 * 1024 * 512 * QUARTER, 7 * MB),
        name="input_terms",
    )(kv, w0, w1)


def dw_kernel(kv, *refs):
    xs, (own, send) = refs[:8], refs[8:]
    x = jnp.concatenate([r[...] for r in xs], axis=0)
    g = lax.dot_general(x, kv[...], TN, preferred_element_type=F32) * SCALING
    own[...] = g[:, :256]
    send[...] = g[:, 256:].astype(BF)


def weight_terms(chunk, kv, xs):
    t = 256
    n = CH // t
    return pl.pallas_call(
        dw_kernel,
        out_shape=[sds((CH, 256), F32), sds((CH, 256), BF)],
        grid=(n,),
        in_specs=[pl.BlockSpec((1024, 512), lambda i: (0, 0))]
        + [pl.BlockSpec((128, t), lambda i: (0, chunk * n + i))] * 8,
        out_specs=[pl.BlockSpec((t, 256), lambda i: (i, 0))] * 2,
        compiler_params=params(24),
        cost_estimate=cost(2 * 1024 * 512 * CH, 5 * MB),
        name="weight_terms",
    )(kv, *xs)


def proj_kernel(*refs):
    xs, (w0, w1), (own, send), acc = refs[:8], refs[8:10], refs[10:12], refs[12]
    i = pl.program_id(0)
    w = jnp.concatenate([w0[...], w1[...]], axis=1)

    @pl.when(i == 0)
    def _():
        acc[...] = jnp.zeros_like(acc)

    for k in range(8):
        rows = slice(128 * k, 128 * k + 128)
        acc[rows] += jnp.dot(xs[k][...], w, preferred_element_type=F32)

    @pl.when(i == pl.num_programs(0) - 1)
    def _():
        own[...] = acc[:, :256] * SCALING
        send[...] = (acc[:, 256:] * SCALING).astype(BF)


def projection(*args):
    t = 512
    wspec = pl.BlockSpec((t, 256), lambda i: (i, 0))
    return pl.pallas_call(
        proj_kernel,
        out_shape=[sds((1024, 256), F32), sds((1024, 256), BF)],
        grid=(QUARTER // t,),
        in_specs=[pl.BlockSpec((128, t), lambda i: (0, i))] * 8 + [wspec] * 2,
        out_specs=[pl.BlockSpec((1024, 256), lambda i: (0, 0))] * 2,
        scratch_shapes=[pltpu.VMEM((1024, 512), F32)],
        compiler_params=params(24),
        cost_estimate=cost(2 * 1024 * 512 * QUARTER, 8 * MB),
        name="projection",
    )(*args)


def proj_sum_kernel(own, got, keep, send):
    for at in range(0, 1024, 64):
        j, o, cr = at // 256, at // 128 % 2, at // 64 % 2
        far = at + 64 - 128 * cr
        total = own[at : at + 64] + got[far : far + 64].astype(F32)
        to = j * 128 + cr * 64
        if o:
            send[to : to + 64] = total.astype(BF)
        else:
            keep[to : to + 64] = total


def projection_sum(own, got):
    return pl.pallas_call(
        proj_sum_kernel,
        out_shape=[sds((512, 256), F32), sds((512, 256), BF)],
        in_specs=[vmem()] * 2,
        out_specs=[vmem()] * 2,
        compiler_params=params(8),
        cost_estimate=cost(0, 2 * MB),
        name="projection_sum",
    )(own, got)


def proj_end_kernel(where, keep, got, keys, values):
    y, c = where[1], where[2]
    for j in range(4):
        for cr in range(2):
            chip = lax.rem(y + j, 4)
            row = pl.multiple_of(chip * 2 * ROWS + (c + cr - 2 * c * cr) * ROWS, ROWS)
            at = j * 128 + cr * ROWS
            total = (keep[at : at + ROWS] + got[at : at + ROWS].astype(F32)).astype(BF)
            keys[pl.ds(row, ROWS), :] = total[:, :COLS]
            values[pl.ds(row, ROWS), :] = total[:, COLS:]


def projection_end(where, keep, got):
    out = pltpu.HBM((512, COLS), BF)
    return pl.pallas_call(
        proj_end_kernel,
        out_shape=[out, out],
        in_specs=[smem()] + [vmem()] * 2,
        out_specs=[vmem()] * 2,
        compiler_params=params(8),
        cost_estimate=cost(0, MB),
        name="projection_end",
    )(where, keep, got)


def sum3_kernel(a, b, c, lo, hi):
    for at, out in ((0, lo), (64, hi)):

        def body(rows):
            far = pl.ds(pl.multiple_of(rows.start + at, 16), rows.size)
            out[rows, :] = (a[far, :].astype(F32) + b[far, :].astype(F32) + c[far, :].astype(F32)).astype(BF)

        by_rows(64, body, 16)


def sum3(a, b, c):
    out = sds((64, QUARTER), BF)
    return pl.pallas_call(
        sum3_kernel,
        out_shape=[out, out],
        in_specs=[vmem()] * 3,
        out_specs=[vmem()] * 2,
        compiler_params=params(8),
        cost_estimate=cost(0, 2 * MB),
        name="sum_terms",
    )(a, b, c)


def join_kernel(where, own, core, z, zc, out):
    f, c = where[0], where[2]
    quarters = (2 * f + c, 2 * f + 1 - c, 2 * (1 - f) + c, 2 * (1 - f) + 1 - c)
    for q, ref in zip(quarters, (own, core, z, zc)):
        out[:, pl.ds(pl.multiple_of(q * QUARTER, QUARTER), QUARTER)] = ref[...]


def join(where, own, core, z, zc):
    return pl.pallas_call(
        join_kernel,
        out_shape=pltpu.HBM((ROWS, D), BF),
        in_specs=[smem()] + [vmem()] * 4,
        out_specs=vmem(),
        compiler_params=params(8),
        cost_estimate=cost(0, 2 * MB),
        name="join_input_grad",
    )(where, own, core, z, zc)


def chunk_specs(chunk):
    n = CH // TILE
    per_quarter = QUARTER // TILE

    def at(s, i, w):
        q = s + w[2] - 2 * s * w[2]
        return (0, q * per_quarter + chunk * n + i, 0)

    whole = pl.BlockSpec((1, TILE, COLS), at)
    term = pl.BlockSpec((TILE, 256), lambda s, i, w: (i, 0))
    moved = pl.BlockSpec((TILE, 256), lambda s, i, w: (s * n + i, 0))
    return (2, n), whole, term, moved


def moved_kernel(pre, own, got, moved):
    def body(rows):
        moved[rows, :] = (pre[rows, :] - learn_rate * own[rows, :]).astype(BF)
        far = pl.ds(pl.multiple_of(rows.start + CH, 128), rows.size)
        moved[far, :] = (pre[far, :] - learn_rate * got[rows, :].astype(F32)).astype(BF)

    by_rows(CH, body)


def moved_chunk(pre, own, got):
    return pl.pallas_call(
        moved_kernel,
        out_shape=sds((2 * CH, 256), BF),
        in_specs=[vmem()] * 3,
        out_specs=vmem(),
        compiler_params=params(8),
        cost_estimate=cost(0, 5 * MB),
        name="moved_weights",
    )(pre, own, got)


def momentum_kernel(where, km, vm, *refs):
    own, got, (nkm, nvm) = refs[:CHUNKS], refs[CHUNKS : 2 * CHUNKS], refs[2 * CHUNKS :]
    s, h = pl.program_id(0), pl.program_id(1)

    def run(g):
        def body(rows):
            nkm[0, rows, :] = momentum_decay * km[0, rows, :] + g[rows, :COLS].astype(F32)
            nvm[0, rows, :] = momentum_decay * vm[0, rows, :] + g[rows, COLS:].astype(F32)

        by_rows(TILE, body)

    for chunk in range(CHUNKS):

        @pl.when((s == 0) & (h == chunk))
        def _():
            run(own[chunk])

        @pl.when((s == 1) & (h == chunk))
        def _():
            run(got[chunk])


def momentum_step(where, km, vm, own, got):
    n = CH // TILE

    def at(s, h, i, w):
        q = s + w[2] - 2 * s * w[2]
        return (0, (q * CHUNKS + h) * n + i, 0)

    whole = pl.BlockSpec((1, TILE, COLS), at)
    terms = [
        pl.BlockSpec(
            (TILE, 256),
            lambda s, h, i, w, kind=kind, chunk=chunk: (jnp.where((s == kind) & (h == chunk), i, 0), 0),
        )
        for kind in range(2)
        for chunk in range(CHUNKS)
    ]
    full = pltpu.HBM((1, HALF, COLS), F32)
    return pl.pallas_call(
        momentum_kernel,
        out_shape=[full, full],
        grid_spec=pltpu.PrefetchScalarGridSpec(
            num_scalar_prefetch=1,
            grid=(2, CHUNKS, n),
            in_specs=[whole] * 2 + terms,
            out_specs=[whole, whole],
        ),
        compiler_params=params(24),
        cost_estimate=cost(0, 11 * MB),
        name="momentum_step",
    )(where, km, vm, *own, *got)


def mean_kernel(where, pre, own, got, partner, *refs):
    nkw, nvw = refs[-2:]
    s = pl.program_id(0)

    def run(g):
        def body(rows):
            mean = 0.5 * ((pre[rows, :] - learn_rate * g[rows, :].astype(F32)) + partner[rows, :].astype(F32))
            nkw[0, rows, :] = mean[:, :COLS]
            nvw[0, rows, :] = mean[:, COLS:]

        by_rows(TILE, body)

    @pl.when(s == 0)
    def _():
        run(own)

    @pl.when(s == 1)
    def _():
        run(got)


def mean(where, chunk, pre, own, got, partner, before):
    grid, whole, term, moved = chunk_specs(chunk)
    full = pltpu.HBM((1, HALF, COLS), F32)
    extra = [] if before is None else list(before)
    return pl.pallas_call(
        mean_kernel,
        out_shape=[full, full],
        grid_spec=pltpu.PrefetchScalarGridSpec(
            num_scalar_prefetch=1,
            grid=grid,
            in_specs=[moved, term, term, moved] + [anywhere()] * len(extra),
            out_specs=[whole, whole],
        ),
        input_output_aliases={5: 0, 6: 1} if extra else {},
        compiler_params=params(24),
        cost_estimate=cost(0, 8 * MB),
        name="average",
    )(where, pre, own, got, partner, *extra)


def to_right(a):
    return lax.ppermute(a, "tensor", [(t, (t + 2) % 8) for t in range(8)])


def to_left(a):
    return lax.ppermute(a, "tensor", [(t, (t + 6) % 8) for t in range(8)])


def to_core(a):
    return lax.ppermute(a, "tensor", [(t, t ^ 1) for t in range(8)])


def to_z(a):
    return lax.ppermute(a, "fsdp", [(0, 1), (1, 0)])


def to_z_core(a):
    return lax.ppermute(a, ("fsdp", "tensor"), [(i, i ^ 9) for i in range(16)])


def to_partner(a, bit):
    n = lax.axis_size("gossip")
    return lax.ppermute(a, "gossip", [(i, i ^ (1 << bit)) for i in range(n)])


def after(value, *others):
    return lax.optimization_barrier((value, others))[0]


def exchange(bit, where, km, vm, kv, pre, terms, xs, w_own, w_core):
    own, send = weight_terms(0, kv, xs)
    got = to_core(send)
    partner = to_partner(moved_chunk(pre[0], own, got), bit)
    o_terms, s_terms = terms[:4], terms[4:]
    o_left = to_left(o_terms[2])
    o_relayed = o_terms[1] + to_right(o_terms[0])
    own1, send = weight_terms(1, after(kv, own), xs)
    got1 = to_core(send)
    p_own, p_send = projection(*xs, w_own, w_core)
    o_right = to_right(after(o_relayed, p_send))
    keep, p_send = projection_sum(p_own, to_core(p_send))
    p_z = to_z(p_send)
    partner1 = to_partner(after(moved_chunk(pre[1], own1, got1), partner, keep), bit)
    keys, values = projection_end(where, keep, p_z)
    o_z, o_zc = sum3(o_terms[3], o_right, o_left)
    z, zc = to_z(o_z), to_z_core(o_zc)
    s_left = to_left(after(s_terms[2] + to_left(after(s_terms[0], o_left)), o_z))
    s_right = to_right(after(s_terms[1], o_right, p_z))
    momenta = momentum_step(after(where, o_z), km, vm, (own, own1), (got, got1))
    weights = mean(where, 0, pre[0], own, got, partner, None)
    s_own, s_core = sum3(after(s_terms[3], momenta, weights), s_right, s_left)
    input_grad = join(where, s_own, to_core(s_core), z, zc)
    weights = mean(where, 1, pre[1], own1, got1, partner1, weights)
    return keys, values, input_grad, *weights, *momenta


def per_device(normed, kc, vc, kw, vw, km, vm, step_index):
    t = lax.axis_index("tensor")
    where = jnp.stack([lax.axis_index("fsdp"), t // 2, t % 2]).astype(jnp.int32)
    levels = lax.axis_size("gossip").bit_length() - 1
    bit = step_index % levels

    normed, kc, vc, kw, vw, km, vm = map(in_hbm, (normed, kc, vc, kw, vw, km, vm))
    kv_own, x_core, z_core, x_own, x_z = split_inputs(where, normed, kc, vc)
    z_core = to_core(z_core)
    b = to_z(jnp.concatenate([x_z, z_core], axis=0))
    a = jnp.concatenate([x_own, to_core(after(x_core, z_core))], axis=0)
    a3, a1 = to_right(a), to_left(a)
    w_own, w_send, *pre = prepare(after(where, a), kw, vw, km, vm)
    a3, a1, b, kv_own, w_own, w_send = lax.optimization_barrier((a3, a1, b, kv_own, w_own, w_send))
    a2 = to_right(a3)
    kv_z = to_z(kv_own)
    b3, b1 = to_right(b), to_left(b)
    b2 = to_left(b1)
    kv = jnp.stack([kv_own.reshape(8, ROWS, 256), kv_z.reshape(8, ROWS, 256)], axis=1).reshape(1024, 256)
    kv = after(kv, a2)
    kv = order_cotangents(where, kv, to_core(kv))
    w_core = to_core(w_send)
    terms = input_terms(kv, w_own, w_core)
    xs = (a, b, a1, b1, a2, b2, a3, b3)
    kv = after(kv, terms[0])
    return lax.switch(
        bit,
        [partial(exchange, k) for k in range(levels)],
        where, km, vm, kv, pre, terms, xs, w_own, w_core,
    )


def solution(mesh):
    rows = P(("gossip", "fsdp", "tensor"), None)
    heads = P(("gossip", "fsdp"), "tensor")
    weight = P("gossip", "fsdp", "tensor")
    return jax.shard_map(
        per_device,
        mesh=mesh,
        in_specs=(rows, heads, heads, weight, weight, weight, weight, P()),
        out_specs=(heads, heads, rows, weight, weight, weight, weight),
        check_vma=False,
    )
```

```python
from functools import partial

import jax
import jax.numpy as jnp
from jax import lax
from jax.experimental import pallas as pl
from jax.experimental.pallas import tpu as pltpu
from jax.sharding import PartitionSpec as P

D = 8192
SCALING = D ** (-0.5)
momentum_decay = 0.9
learn_rate = 0.5

F32 = jnp.float32
BF = jnp.bfloat16
HALF = 4096
QUARTER = 2048
CHUNKS = 2
CH = QUARTER // CHUNKS
ROWS = 64
TOK = 512
COLS = 128
TILE = 1024

MB = 1024 * 1024


def sds(shape, dtype):
    return jax.ShapeDtypeStruct(shape, dtype)


def params(mib):
    return pltpu.CompilerParams(vmem_limit_bytes=mib * MB)


def cost(flops, nbytes):
    return pl.CostEstimate(flops=flops // 1000, bytes_accessed=nbytes // 1000, transcendentals=0)


def in_hbm(x):
    return pltpu.with_memory_space_constraint(x, pltpu.HBM)


def by_rows(rows, body, size=128):
    @pl.loop(0, rows // size)
    def _(i):
        body(pl.ds(pl.multiple_of(i * size, size), size))


def smem():
    return pl.BlockSpec(memory_space=pltpu.SMEM)


def vmem():
    return pl.BlockSpec(memory_space=pltpu.VMEM)


def copies(pairs, sems):
    started = [pltpu.make_async_copy(src, dst, sems.at[i]) for i, (src, dst) in enumerate(pairs)]
    for copy in started:
        copy.start()
    for copy in started:
        copy.wait()


def anywhere():
    return pl.BlockSpec(memory_space=pl.ANY)


def split_kernel(where, x, k, v, kv, core_own, core_other, own, other, sems):
    core = (core_own, core_other)
    f, c = where[0], where[2]
    pairs = []
    for g, out in enumerate((own, other)):
        q = 2 * (f + g - 2 * f * g)
        start = pl.multiple_of((q + 1 - c) * QUARTER, QUARTER)
        pairs.append((x.at[:, pl.ds(start, QUARTER)], core[g]))
        start = pl.multiple_of((q + c) * QUARTER, QUARTER)
        pairs.append((x.at[:, pl.ds(start, QUARTER)], out))
    pairs += [(k, kv.at[:, :COLS]), (v, kv.at[:, COLS:])]
    copies(pairs, sems)


def split_inputs(where, x, k, v):
    piece = sds((ROWS, QUARTER), BF)
    return pl.pallas_call(
        split_kernel,
        out_shape=[sds((TOK, 2 * COLS), BF), piece, piece, piece, piece],
        in_specs=[smem()] + [anywhere()] * 3,
        out_specs=[anywhere()] * 5,
        scratch_shapes=[pltpu.SemaphoreType.DMA((6,))],
        compiler_params=params(4),
        cost_estimate=cost(0, 2_600_000),
        name="split_inputs",
    )(where, x, k, v)


def prepare_kernel(where, kw, vw, km, vm, w_own, w_send, *pre):
    h, s = pl.program_id(0), pl.program_id(1)
    halves = ((kw, km, slice(0, COLS)), (vw, vm, slice(COLS, 2 * COLS)))
    for chunk in range(CHUNKS):
        for kind, rounded in ((0, w_own), (1, w_send)):

            @pl.when((h == chunk) & (s == kind))
            def _():
                def body(rows):
                    for w, m, cols in halves:
                        value = w[0, rows, :]
                        pre[chunk][rows, cols] = value - (learn_rate * momentum_decay) * m[0, rows, :]
                        rounded[rows, cols] = value.astype(BF)

                by_rows(TILE, body)


def prepare(where, kw, vw, km, vm):
    n = CH // TILE

    def at(h, s, i, w):
        q = s + w[2] - 2 * s * w[2]
        return (0, (q * CHUNKS + h) * n + i, 0)

    def chunk_at(chunk):
        def index(h, s, i, w):
            inside = s * n + i
            return (jnp.where(h == chunk, inside, jnp.where(h < chunk, 0, 2 * n - 1)), 0)

        return index

    whole = pl.BlockSpec((1, TILE, COLS), at)
    tile = (TILE, 256)
    return pl.pallas_call(
        prepare_kernel,
        out_shape=[sds((QUARTER, 256), BF)] * 2 + [sds((2 * CH, 256), F32)] * CHUNKS,
        grid_spec=pltpu.PrefetchScalarGridSpec(
            num_scalar_prefetch=1,
            grid=(CHUNKS, 2, n),
            in_specs=[whole] * 4,
            out_specs=[
                pl.BlockSpec(tile, lambda h, s, i, w: (h * n + jnp.where(s == 0, i, n - 1), 0)),
                pl.BlockSpec(tile, lambda h, s, i, w: (h * n + jnp.where(s == 1, i, 0), 0)),
            ]
            + [pl.BlockSpec(tile, chunk_at(chunk)) for chunk in range(CHUNKS)],
        ),
        compiler_params=params(24),
        cost_estimate=cost(0, 14 * MB),
        name="prepare_weights",
    )(where, kw, vw, km, vm)


def order_kernel(where, own, core, out):
    y, c = where[1], where[2]
    for j in range(4):
        for cr in range(2):
            t = 2 * lax.rem(y + j, 4) + (c + cr - 2 * c * cr)
            for g in range(2):
                row = pl.multiple_of(t * 2 * ROWS + g * ROWS, ROWS)
                to = j * 256 + g * 128 + cr * ROWS
                out[to : to + ROWS, : 2 * COLS] = own[pl.ds(row, ROWS), :]
                out[to : to + ROWS, 2 * COLS :] = core[pl.ds(row, ROWS), :]


def order_cotangents(where, own, core):
    return pl.pallas_call(
        order_kernel,
        out_shape=sds((1024, 512), BF),
        in_specs=[smem()] + [vmem()] * 2,
        out_specs=vmem(),
        compiler_params=params(8),
        cost_estimate=cost(0, 2 * MB),
        name="order_cotangents",
    )(where, own, core)


NT = (((1,), (1,)), ((), ()))
TN = (((0,), (0,)), ((), ()))
DXT = 1024


def dx_kernel(kv, w0, w1, *outs):
    part = lax.dot_general(kv[:, :256], w0[...], NT, preferred_element_type=F32)
    part += lax.dot_general(kv[:, 256:], w1[...], NT, preferred_element_type=F32)
    part = (part * SCALING).astype(BF)
    for g in range(2):
        for out, chip in zip(outs[4 * g : 4 * g + 4], (2, 1, 3, 0)):
            base = 256 * chip + 128 * (1 - g)
            out[...] = part[base : base + 128]


def input_terms(kv, w0, w1):
    spec = pl.BlockSpec((128, DXT), lambda i: (0, i))
    wspec = pl.BlockSpec((DXT, 256), lambda i: (i, 0))
    return pl.pallas_call(
        dx_kernel,
        out_shape=[sds((128, QUARTER), BF)] * 8,
        grid=(QUARTER // DXT,),
        in_specs=[pl.BlockSpec((1024, 512), lambda i: (0, 0)), wspec, wspec],
        out_specs=[spec] * 8,
        compiler_params=params(24),
        cost_estimate=cost(2 * 1024 * 512 * QUARTER, 7 * MB),
        name="input_terms",
    )(kv, w0, w1)


def dw_kernel(kv, *refs):
    xs, (own, send) = refs[:8], refs[8:]
    x = jnp.concatenate([r[...] for r in xs], axis=0)
    g = lax.dot_general(x, kv[...], TN, preferred_element_type=F32) * SCALING
    own[...] = g[:, :256]
    send[...] = g[:, 256:].astype(BF)


def weight_terms(chunk, kv, xs):
    t = 512
    n = CH // t
    return pl.pallas_call(
        dw_kernel,
        out_shape=[sds((CH, 256), F32), sds((CH, 256), BF)],
        grid=(n,),
        in_specs=[pl.BlockSpec((1024, 512), lambda i: (0, 0))]
        + [pl.BlockSpec((128, t), lambda i: (0, chunk * n + i))] * 8,
        out_specs=[pl.BlockSpec((t, 256), lambda i: (i, 0))] * 2,
        compiler_params=params(24),
        cost_estimate=cost(2 * 1024 * 512 * CH, 5 * MB),
        name="weight_terms",
    )(kv, *xs)


def proj_kernel(*refs):
    xs, (w0, w1), (own, send), acc = refs[:8], refs[8:10], refs[10:12], refs[12]
    i = pl.program_id(0)
    w = jnp.concatenate([w0[...], w1[...]], axis=1)

    @pl.when(i == 0)
    def _():
        acc[...] = jnp.zeros_like(acc)

    for k in range(8):
        rows = slice(128 * k, 128 * k + 128)
        acc[rows] += jnp.dot(xs[k][...], w, preferred_element_type=F32)

    @pl.when(i == pl.num_programs(0) - 1)
    def _():
        own[...] = acc[:, :256] * SCALING
        send[...] = (acc[:, 256:] * SCALING).astype(BF)


def projection(*args):
    t = 512
    wspec = pl.BlockSpec((t, 256), lambda i: (i, 0))
    return pl.pallas_call(
        proj_kernel,
        out_shape=[sds((1024, 256), F32), sds((1024, 256), BF)],
        grid=(QUARTER // t,),
        in_specs=[pl.BlockSpec((128, t), lambda i: (0, i))] * 8 + [wspec] * 2,
        out_specs=[pl.BlockSpec((1024, 256), lambda i: (0, 0))] * 2,
        scratch_shapes=[pltpu.VMEM((1024, 512), F32)],
        compiler_params=params(24),
        cost_estimate=cost(2 * 1024 * 512 * QUARTER, 8 * MB),
        name="projection",
    )(*args)


def proj_sum_kernel(own, got, keep, send):
    for at in range(0, 1024, 64):
        j, o, cr = at // 256, at // 128 % 2, at // 64 % 2
        far = at + 64 - 128 * cr
        total = own[at : at + 64] + got[far : far + 64].astype(F32)
        to = j * 128 + cr * 64
        if o:
            send[to : to + 64] = total.astype(BF)
        else:
            keep[to : to + 64] = total


def projection_sum(own, got):
    return pl.pallas_call(
        proj_sum_kernel,
        out_shape=[sds((512, 256), F32), sds((512, 256), BF)],
        in_specs=[vmem()] * 2,
        out_specs=[vmem()] * 2,
        compiler_params=params(8),
        cost_estimate=cost(0, 2 * MB),
        name="projection_sum",
    )(own, got)


def proj_end_kernel(where, keep, got, keys, values):
    y, c = where[1], where[2]
    for j in range(4):
        for cr in range(2):
            chip = lax.rem(y + j, 4)
            row = pl.multiple_of(chip * 2 * ROWS + (c + cr - 2 * c * cr) * ROWS, ROWS)
            at = j * 128 + cr * ROWS
            total = (keep[at : at + ROWS] + got[at : at + ROWS].astype(F32)).astype(BF)
            keys[pl.ds(row, ROWS), :] = total[:, :COLS]
            values[pl.ds(row, ROWS), :] = total[:, COLS:]


def projection_end(where, keep, got):
    out = pltpu.HBM((512, COLS), BF)
    return pl.pallas_call(
        proj_end_kernel,
        out_shape=[out, out],
        in_specs=[smem()] + [vmem()] * 2,
        out_specs=[vmem()] * 2,
        compiler_params=params(8),
        cost_estimate=cost(0, MB),
        name="projection_end",
    )(where, keep, got)


def sum3_kernel(a, b, c, lo, hi):
    for at, out in ((0, lo), (64, hi)):

        def body(rows):
            far = pl.ds(pl.multiple_of(rows.start + at, 16), rows.size)
            out[rows, :] = (a[far, :].astype(F32) + b[far, :].astype(F32) + c[far, :].astype(F32)).astype(BF)

        by_rows(64, body, 16)


def sum3(a, b, c):
    out = sds((64, QUARTER), BF)
    return pl.pallas_call(
        sum3_kernel,
        out_shape=[out, out],
        in_specs=[vmem()] * 3,
        out_specs=[vmem()] * 2,
        compiler_params=params(8),
        cost_estimate=cost(0, 2 * MB),
        name="sum_terms",
    )(a, b, c)


def join_kernel(where, own, core, z, zc, out):
    f, c = where[0], where[2]
    quarters = (2 * f + c, 2 * f + 1 - c, 2 * (1 - f) + c, 2 * (1 - f) + 1 - c)
    for q, ref in zip(quarters, (own, core, z, zc)):
        out[:, pl.ds(pl.multiple_of(q * QUARTER, QUARTER), QUARTER)] = ref[...]


def join(where, own, core, z, zc):
    return pl.pallas_call(
        join_kernel,
        out_shape=pltpu.HBM((ROWS, D), BF),
        in_specs=[smem()] + [vmem()] * 4,
        out_specs=vmem(),
        compiler_params=params(8),
        cost_estimate=cost(0, 2 * MB),
        name="join_input_grad",
    )(where, own, core, z, zc)


def chunk_specs(chunk):
    n = CH // TILE
    per_quarter = QUARTER // TILE

    def at(s, i, w):
        q = s + w[2] - 2 * s * w[2]
        return (0, q * per_quarter + chunk * n + i, 0)

    whole = pl.BlockSpec((1, TILE, COLS), at)
    term = pl.BlockSpec((TILE, 256), lambda s, i, w: (i, 0))
    moved = pl.BlockSpec((TILE, 256), lambda s, i, w: (s * n + i, 0))
    return (2, n), whole, term, moved


def moved_kernel(pre, own, got, moved):
    def body(rows):
        moved[rows, :] = (pre[rows, :] - learn_rate * own[rows, :]).astype(BF)
        far = pl.ds(pl.multiple_of(rows.start + CH, 128), rows.size)
        moved[far, :] = (pre[far, :] - learn_rate * got[rows, :].astype(F32)).astype(BF)

    by_rows(CH, body)


def moved_chunk(pre, own, got):
    return pl.pallas_call(
        moved_kernel,
        out_shape=sds((2 * CH, 256), BF),
        in_specs=[vmem()] * 3,
        out_specs=vmem(),
        compiler_params=params(8),
        cost_estimate=cost(0, 5 * MB),
        name="moved_weights",
    )(pre, own, got)


def momentum_kernel(where, km, vm, *refs):
    own, got, (nkm, nvm) = refs[:CHUNKS], refs[CHUNKS : 2 * CHUNKS], refs[2 * CHUNKS :]
    s, h = pl.program_id(0), pl.program_id(1)

    def run(g):
        def body(rows):
            nkm[0, rows, :] = momentum_decay * km[0, rows, :] + g[rows, :COLS].astype(F32)
            nvm[0, rows, :] = momentum_decay * vm[0, rows, :] + g[rows, COLS:].astype(F32)

        by_rows(TILE, body)

    for chunk in range(CHUNKS):

        @pl.when((s == 0) & (h == chunk))
        def _():
            run(own[chunk])

        @pl.when((s == 1) & (h == chunk))
        def _():
            run(got[chunk])


def momentum_step(where, km, vm, own, got):
    n = CH // TILE

    def at(s, h, i, w):
        q = s + w[2] - 2 * s * w[2]
        return (0, (q * CHUNKS + h) * n + i, 0)

    whole = pl.BlockSpec((1, TILE, COLS), at)
    terms = [
        pl.BlockSpec(
            (TILE, 256),
            lambda s, h, i, w, kind=kind, chunk=chunk: (jnp.where((s == kind) & (h == chunk), i, 0), 0),
        )
        for kind in range(2)
        for chunk in range(CHUNKS)
    ]
    full = pltpu.HBM((1, HALF, COLS), F32)
    return pl.pallas_call(
        momentum_kernel,
        out_shape=[full, full],
        grid_spec=pltpu.PrefetchScalarGridSpec(
            num_scalar_prefetch=1,
            grid=(2, CHUNKS, n),
            in_specs=[whole] * 2 + terms,
            out_specs=[whole, whole],
        ),
        compiler_params=params(24),
        cost_estimate=cost(0, 11 * MB),
        name="momentum_step",
    )(where, km, vm, *own, *got)


def mean_kernel(where, pre, own, got, partner, *refs):
    nkw, nvw = refs[-2:]
    s = pl.program_id(0)

    def run(g):
        def body(rows):
            mean = 0.5 * ((pre[rows, :] - learn_rate * g[rows, :].astype(F32)) + partner[rows, :].astype(F32))
            nkw[0, rows, :] = mean[:, :COLS]
            nvw[0, rows, :] = mean[:, COLS:]

        by_rows(TILE, body)

    @pl.when(s == 0)
    def _():
        run(own)

    @pl.when(s == 1)
    def _():
        run(got)


def mean(where, chunk, pre, own, got, partner, before):
    grid, whole, term, moved = chunk_specs(chunk)
    full = pltpu.HBM((1, HALF, COLS), F32)
    extra = [] if before is None else list(before)
    return pl.pallas_call(
        mean_kernel,
        out_shape=[full, full],
        grid_spec=pltpu.PrefetchScalarGridSpec(
            num_scalar_prefetch=1,
            grid=grid,
            in_specs=[moved, term, term, moved] + [anywhere()] * len(extra),
            out_specs=[whole, whole],
        ),
        input_output_aliases={5: 0, 6: 1} if extra else {},
        compiler_params=params(24),
        cost_estimate=cost(0, 8 * MB),
        name="average",
    )(where, pre, own, got, partner, *extra)


def to_right(a):
    return lax.ppermute(a, "tensor", [(t, (t + 2) % 8) for t in range(8)])


def to_left(a):
    return lax.ppermute(a, "tensor", [(t, (t + 6) % 8) for t in range(8)])


def to_core(a):
    return lax.ppermute(a, "tensor", [(t, t ^ 1) for t in range(8)])


def to_z(a):
    return lax.ppermute(a, "fsdp", [(0, 1), (1, 0)])


def to_z_core(a):
    return lax.ppermute(a, ("fsdp", "tensor"), [(i, i ^ 9) for i in range(16)])


def to_partner(a, bit):
    n = lax.axis_size("gossip")
    return lax.ppermute(a, "gossip", [(i, i ^ (1 << bit)) for i in range(n)])


def after(value, *others):
    return lax.optimization_barrier((value, others))[0]


def exchange(bit, where, km, vm, kv, pre, terms, xs, w_own, w_core):
    own, send = weight_terms(0, kv, xs)
    got = to_core(send)
    partner = to_partner(moved_chunk(pre[0], own, got), bit)
    o_terms, s_terms = terms[:4], terms[4:]
    o_left = to_left(o_terms[2])
    o_relayed = o_terms[1] + to_right(o_terms[0])
    own1, send = weight_terms(1, after(kv, own), xs)
    got1 = to_core(send)
    p_own, p_send = projection(*xs, w_own, w_core)
    o_right = to_right(after(o_relayed, p_send))
    keep, p_send = projection_sum(p_own, to_core(p_send))
    p_z = to_z(p_send)
    partner1 = to_partner(after(moved_chunk(pre[1], own1, got1), keep), bit)
    keys, values = projection_end(where, keep, p_z)
    o_z, o_zc = sum3(o_terms[3], o_right, o_left)
    z, zc = to_z(o_z), to_z_core(o_zc)
    weights = mean(where, 0, pre[0], own, got, partner, None)
    s_left = to_left(after(s_terms[2] + to_left(after(s_terms[0], o_left)), o_z, weights[0]))
    s_right = to_right(after(s_terms[1], o_right, p_z if bit else p_send))
    momenta = momentum_step(after(where, o_z), km, vm, (own, own1), (got, got1))
    s_own, s_core = sum3(after(s_terms[3], momenta, weights), s_right, s_left)
    parts = (s_own, to_core(s_core), z, zc)
    if bit:
        input_grad = join(where, *parts)
        partner1 = after(partner1, input_grad)
    weights = mean(where, 1, pre[1], own1, got1, partner1, weights)
    if not bit:
        input_grad = join(where, *after(parts, weights[0]))
    return keys, values, input_grad, *weights, *momenta


def per_device(normed, kc, vc, kw, vw, km, vm, step_index):
    t = lax.axis_index("tensor")
    where = jnp.stack([lax.axis_index("fsdp"), t // 2, t % 2]).astype(jnp.int32)
    levels = lax.axis_size("gossip").bit_length() - 1
    bit = step_index % levels

    normed, kc, vc, kw, vw, km, vm = map(in_hbm, (normed, kc, vc, kw, vw, km, vm))
    kv_own, x_core, z_core, x_own, x_z = split_inputs(where, normed, kc, vc)
    z_core = to_core(z_core)
    b = to_z(jnp.concatenate([x_z, z_core], axis=0))
    a = jnp.concatenate([x_own, to_core(after(x_core, z_core))], axis=0)
    a3, a1 = to_right(a), to_left(a)
    w_own, w_send, *pre = prepare(after(where, a), kw, vw, km, vm)
    a3, b, w_own, w_send = lax.optimization_barrier((a3, b, w_own, w_send))
    a1, kv_own = lax.optimization_barrier((a1, kv_own))
    a2 = to_right(a3)
    kv_z = to_z(kv_own)
    b3, b1 = to_right(b), to_left(b)
    b2 = to_left(b1)
    kv = jnp.stack([kv_own.reshape(8, ROWS, 256), kv_z.reshape(8, ROWS, 256)], axis=1).reshape(1024, 256)
    kv = after(kv, a2)
    kv = order_cotangents(where, kv, to_core(kv))
    w_core = to_core(w_send)
    terms = input_terms(kv, w_own, w_core)
    xs = (a, b, a1, b1, a2, b2, a3, b3)
    kv = after(kv, terms[0])
    return lax.switch(
        bit,
        [partial(exchange, k) for k in range(levels)],
        where, km, vm, kv, pre, terms, xs, w_own, w_core,
    )


def solution(mesh):
    rows = P(("gossip", "fsdp", "tensor"), None)
    heads = P(("gossip", "fsdp"), "tensor")
    weight = P("gossip", "fsdp", "tensor")
    return jax.shard_map(
        per_device,
        mesh=mesh,
        in_specs=(rows, heads, heads, weight, weight, weight, weight, P()),
        out_specs=(heads, heads, rows, weight, weight, weight, weight),
        check_vma=False,
    )
```

```python
from functools import partial

import jax
import jax.numpy as jnp
from jax import lax
from jax.experimental import pallas as pl
from jax.experimental.pallas import tpu as pltpu
from jax.sharding import PartitionSpec as P

D = 8192
SCALING = D ** (-0.5)
momentum_decay = 0.9
learn_rate = 0.5

F32 = jnp.float32
BF = jnp.bfloat16
HALF = 4096
QUARTER = 2048
CHUNKS = 2
CH = QUARTER // CHUNKS
ROWS = 64
TOK = 512
COLS = 128
TILE = 1024

MB = 1024 * 1024


def sds(shape, dtype):
    return jax.ShapeDtypeStruct(shape, dtype)


def params(mib):
    return pltpu.CompilerParams(vmem_limit_bytes=mib * MB)


def cost(flops, nbytes):
    return pl.CostEstimate(flops=flops // 1000, bytes_accessed=nbytes // 1000, transcendentals=0)


def in_hbm(x):
    return pltpu.with_memory_space_constraint(x, pltpu.HBM)


def by_rows(rows, body, size=128):
    @pl.loop(0, rows // size)
    def _(i):
        body(pl.ds(pl.multiple_of(i * size, size), size))


def smem():
    return pl.BlockSpec(memory_space=pltpu.SMEM)


def vmem():
    return pl.BlockSpec(memory_space=pltpu.VMEM)


def copies(pairs, sems):
    started = [pltpu.make_async_copy(src, dst, sems.at[i]) for i, (src, dst) in enumerate(pairs)]
    for copy in started:
        copy.start()
    for copy in started:
        copy.wait()


def anywhere():
    return pl.BlockSpec(memory_space=pl.ANY)


def split_kernel(where, x, k, v, kv, core_own, core_other, own, other, sems):
    core = (core_own, core_other)
    f, c = where[0], where[2]
    pairs = []
    for g, out in enumerate((own, other)):
        q = 2 * (f + g - 2 * f * g)
        start = pl.multiple_of((q + 1 - c) * QUARTER, QUARTER)
        pairs.append((x.at[:, pl.ds(start, QUARTER)], core[g]))
        start = pl.multiple_of((q + c) * QUARTER, QUARTER)
        pairs.append((x.at[:, pl.ds(start, QUARTER)], out))
    pairs += [(k, kv.at[:, :COLS]), (v, kv.at[:, COLS:])]
    copies(pairs, sems)


def split_inputs(where, x, k, v):
    piece = sds((ROWS, QUARTER), BF)
    return pl.pallas_call(
        split_kernel,
        out_shape=[sds((TOK, 2 * COLS), BF), piece, piece, piece, piece],
        in_specs=[smem()] + [anywhere()] * 3,
        out_specs=[anywhere()] * 5,
        scratch_shapes=[pltpu.SemaphoreType.DMA((6,))],
        compiler_params=params(4),
        cost_estimate=cost(0, 2_600_000),
        name="split_inputs",
    )(where, x, k, v)


def prepare_kernel(where, kw, vw, km, vm, w_own, w_send, *pre):
    h, s = pl.program_id(0), pl.program_id(1)
    halves = ((kw, km, slice(0, COLS)), (vw, vm, slice(COLS, 2 * COLS)))
    for chunk in range(CHUNKS):
        for kind, rounded in ((0, w_own), (1, w_send)):

            @pl.when((h == chunk) & (s == kind))
            def _():
                def body(rows):
                    for w, m, cols in halves:
                        value = w[0, rows, :]
                        pre[chunk][rows, cols] = value - (learn_rate * momentum_decay) * m[0, rows, :]
                        rounded[rows, cols] = value.astype(BF)

                by_rows(TILE, body)


def prepare(where, kw, vw, km, vm):
    n = CH // TILE

    def at(h, s, i, w):
        q = s + w[2] - 2 * s * w[2]
        return (0, (q * CHUNKS + h) * n + i, 0)

    def chunk_at(chunk):
        def index(h, s, i, w):
            inside = s * n + i
            return (jnp.where(h == chunk, inside, jnp.where(h < chunk, 0, 2 * n - 1)), 0)

        return index

    whole = pl.BlockSpec((1, TILE, COLS), at)
    tile = (TILE, 256)
    return pl.pallas_call(
        prepare_kernel,
        out_shape=[sds((QUARTER, 256), BF)] * 2 + [sds((2 * CH, 256), F32)] * CHUNKS,
        grid_spec=pltpu.PrefetchScalarGridSpec(
            num_scalar_prefetch=1,
            grid=(CHUNKS, 2, n),
            in_specs=[whole] * 4,
            out_specs=[
                pl.BlockSpec(tile, lambda h, s, i, w: (h * n + jnp.where(s == 0, i, n - 1), 0)),
                pl.BlockSpec(tile, lambda h, s, i, w: (h * n + jnp.where(s == 1, i, 0), 0)),
            ]
            + [pl.BlockSpec(tile, chunk_at(chunk)) for chunk in range(CHUNKS)],
        ),
        compiler_params=params(24),
        cost_estimate=cost(0, 14 * MB),
        name="prepare_weights",
    )(where, kw, vw, km, vm)


def order_kernel(where, own, core, out):
    y, c = where[1], where[2]
    for j in range(4):
        for cr in range(2):
            t = 2 * lax.rem(y + j, 4) + (c + cr - 2 * c * cr)
            for g in range(2):
                row = pl.multiple_of(t * 2 * ROWS + g * ROWS, ROWS)
                to = j * 256 + g * 128 + cr * ROWS
                out[to : to + ROWS, : 2 * COLS] = own[pl.ds(row, ROWS), :]
                out[to : to + ROWS, 2 * COLS :] = core[pl.ds(row, ROWS), :]


def order_cotangents(where, own, core):
    return pl.pallas_call(
        order_kernel,
        out_shape=sds((1024, 512), BF),
        in_specs=[smem()] + [vmem()] * 2,
        out_specs=vmem(),
        compiler_params=params(8),
        cost_estimate=cost(0, 2 * MB),
        name="order_cotangents",
    )(where, own, core)


NT = (((1,), (1,)), ((), ()))
TN = (((0,), (0,)), ((), ()))
DXT = 1024


def dx_kernel(kv, w0, w1, *outs):
    part = lax.dot_general(kv[:, :256], w0[...], NT, preferred_element_type=F32)
    part += lax.dot_general(kv[:, 256:], w1[...], NT, preferred_element_type=F32)
    part = (part * SCALING).astype(BF)
    for g in range(2):
        for out, chip in zip(outs[4 * g : 4 * g + 4], (2, 1, 3, 0)):
            base = 256 * chip + 128 * (1 - g)
            out[...] = part[base : base + 128]


def input_terms(kv, w0, w1):
    spec = pl.BlockSpec((128, DXT), lambda i: (0, i))
    wspec = pl.BlockSpec((DXT, 256), lambda i: (i, 0))
    return pl.pallas_call(
        dx_kernel,
        out_shape=[sds((128, QUARTER), BF)] * 8,
        grid=(QUARTER // DXT,),
        in_specs=[pl.BlockSpec((1024, 512), lambda i: (0, 0)), wspec, wspec],
        out_specs=[spec] * 8,
        compiler_params=params(24),
        cost_estimate=cost(2 * 1024 * 512 * QUARTER, 7 * MB),
        name="input_terms",
    )(kv, w0, w1)


def dw_kernel(kv, *refs):
    xs, (own, send) = refs[:8], refs[8:]
    x = jnp.concatenate([r[...] for r in xs], axis=0)
    g = lax.dot_general(x, kv[...], TN, preferred_element_type=F32) * SCALING
    own[...] = g[:, :256]
    send[...] = g[:, 256:].astype(BF)


def weight_terms(chunk, kv, xs):
    t = 512
    n = CH // t
    return pl.pallas_call(
        dw_kernel,
        out_shape=[sds((CH, 256), F32), sds((CH, 256), BF)],
        grid=(n,),
        in_specs=[pl.BlockSpec((1024, 512), lambda i: (0, 0))]
        + [pl.BlockSpec((128, t), lambda i: (0, chunk * n + i))] * 8,
        out_specs=[pl.BlockSpec((t, 256), lambda i: (i, 0))] * 2,
        compiler_params=params(24),
        cost_estimate=cost(2 * 1024 * 512 * CH, 5 * MB),
        name="weight_terms",
    )(kv, *xs)


def proj_kernel(*refs):
    xs, (w0, w1), (own, send), acc = refs[:8], refs[8:10], refs[10:12], refs[12]
    i = pl.program_id(0)
    w = jnp.concatenate([w0[...], w1[...]], axis=1)

    @pl.when(i == 0)
    def _():
        acc[...] = jnp.zeros_like(acc)

    for k in range(8):
        rows = slice(128 * k, 128 * k + 128)
        acc[rows] += jnp.dot(xs[k][...], w, preferred_element_type=F32)

    @pl.when(i == pl.num_programs(0) - 1)
    def _():
        own[...] = acc[:, :256] * SCALING
        send[...] = (acc[:, 256:] * SCALING).astype(BF)


def projection(*args):
    t = 512
    wspec = pl.BlockSpec((t, 256), lambda i: (i, 0))
    return pl.pallas_call(
        proj_kernel,
        out_shape=[sds((1024, 256), F32), sds((1024, 256), BF)],
        grid=(QUARTER // t,),
        in_specs=[pl.BlockSpec((128, t), lambda i: (0, i))] * 8 + [wspec] * 2,
        out_specs=[pl.BlockSpec((1024, 256), lambda i: (0, 0))] * 2,
        scratch_shapes=[pltpu.VMEM((1024, 512), F32)],
        compiler_params=params(24),
        cost_estimate=cost(2 * 1024 * 512 * QUARTER, 8 * MB),
        name="projection",
    )(*args)


def proj_sum_kernel(own, got, keep, send):
    for at in range(0, 1024, 64):
        j, o, cr = at // 256, at // 128 % 2, at // 64 % 2
        far = at + 64 - 128 * cr
        total = own[at : at + 64] + got[far : far + 64].astype(F32)
        to = j * 128 + cr * 64
        if o:
            send[to : to + 64] = total.astype(BF)
        else:
            keep[to : to + 64] = total


def projection_sum(own, got):
    return pl.pallas_call(
        proj_sum_kernel,
        out_shape=[sds((512, 256), F32), sds((512, 256), BF)],
        in_specs=[vmem()] * 2,
        out_specs=[vmem()] * 2,
        compiler_params=params(8),
        cost_estimate=cost(0, 2 * MB),
        name="projection_sum",
    )(own, got)


def proj_end_kernel(where, keep, got, keys, values):
    y, c = where[1], where[2]
    for j in range(4):
        for cr in range(2):
            chip = lax.rem(y + j, 4)
            row = pl.multiple_of(chip * 2 * ROWS + (c + cr - 2 * c * cr) * ROWS, ROWS)
            at = j * 128 + cr * ROWS
            total = (keep[at : at + ROWS] + got[at : at + ROWS].astype(F32)).astype(BF)
            keys[pl.ds(row, ROWS), :] = total[:, :COLS]
            values[pl.ds(row, ROWS), :] = total[:, COLS:]


def projection_end(where, keep, got):
    out = pltpu.HBM((512, COLS), BF)
    return pl.pallas_call(
        proj_end_kernel,
        out_shape=[out, out],
        in_specs=[smem()] + [vmem()] * 2,
        out_specs=[vmem()] * 2,
        compiler_params=params(8),
        cost_estimate=cost(0, MB),
        name="projection_end",
    )(where, keep, got)


def sum3_kernel(a, b, c, lo, hi):
    for at, out in ((0, lo), (64, hi)):

        def body(rows):
            far = pl.ds(pl.multiple_of(rows.start + at, 16), rows.size)
            out[rows, :] = (a[far, :].astype(F32) + b[far, :].astype(F32) + c[far, :].astype(F32)).astype(BF)

        by_rows(64, body, 16)


def sum3(a, b, c):
    out = sds((64, QUARTER), BF)
    return pl.pallas_call(
        sum3_kernel,
        out_shape=[out, out],
        in_specs=[vmem()] * 3,
        out_specs=[vmem()] * 2,
        compiler_params=params(8),
        cost_estimate=cost(0, 2 * MB),
        name="sum_terms",
    )(a, b, c)


def join_kernel(where, own, core, z, zc, out):
    f, c = where[0], where[2]
    quarters = (2 * f + c, 2 * f + 1 - c, 2 * (1 - f) + c, 2 * (1 - f) + 1 - c)
    for q, ref in zip(quarters, (own, core, z, zc)):
        out[:, pl.ds(pl.multiple_of(q * QUARTER, QUARTER), QUARTER)] = ref[...]


def join(where, own, core, z, zc):
    return pl.pallas_call(
        join_kernel,
        out_shape=pltpu.HBM((ROWS, D), BF),
        in_specs=[smem()] + [vmem()] * 4,
        out_specs=vmem(),
        compiler_params=params(8),
        cost_estimate=cost(0, 2 * MB),
        name="join_input_grad",
    )(where, own, core, z, zc)


def chunk_specs(chunk):
    n = CH // TILE
    per_quarter = QUARTER // TILE

    def at(s, i, w):
        q = s + w[2] - 2 * s * w[2]
        return (0, q * per_quarter + chunk * n + i, 0)

    whole = pl.BlockSpec((1, TILE, COLS), at)
    term = pl.BlockSpec((TILE, 256), lambda s, i, w: (i, 0))
    moved = pl.BlockSpec((TILE, 256), lambda s, i, w: (s * n + i, 0))
    return (2, n), whole, term, moved


def moved_kernel(pre, own, got, moved):
    def body(rows):
        moved[rows, :] = (pre[rows, :] - learn_rate * own[rows, :]).astype(BF)
        far = pl.ds(pl.multiple_of(rows.start + CH, 128), rows.size)
        moved[far, :] = (pre[far, :] - learn_rate * got[rows, :].astype(F32)).astype(BF)

    by_rows(CH, body)


def moved_chunk(pre, own, got):
    return pl.pallas_call(
        moved_kernel,
        out_shape=sds((2 * CH, 256), BF),
        in_specs=[vmem()] * 3,
        out_specs=vmem(),
        compiler_params=params(8),
        cost_estimate=cost(0, 5 * MB),
        name="moved_weights",
    )(pre, own, got)


def momentum_kernel(where, km, vm, *refs):
    own, got, (nkm, nvm) = refs[:CHUNKS], refs[CHUNKS : 2 * CHUNKS], refs[2 * CHUNKS :]
    s, h = pl.program_id(0), pl.program_id(1)

    def run(g):
        def body(rows):
            nkm[0, rows, :] = momentum_decay * km[0, rows, :] + g[rows, :COLS].astype(F32)
            nvm[0, rows, :] = momentum_decay * vm[0, rows, :] + g[rows, COLS:].astype(F32)

        by_rows(TILE, body)

    for chunk in range(CHUNKS):

        @pl.when((s == 0) & (h == chunk))
        def _():
            run(own[chunk])

        @pl.when((s == 1) & (h == chunk))
        def _():
            run(got[chunk])


def momentum_step(where, km, vm, own, got):
    n = CH // TILE

    def at(s, h, i, w):
        q = s + w[2] - 2 * s * w[2]
        return (0, (q * CHUNKS + h) * n + i, 0)

    whole = pl.BlockSpec((1, TILE, COLS), at)
    terms = [
        pl.BlockSpec(
            (TILE, 256),
            lambda s, h, i, w, kind=kind, chunk=chunk: (jnp.where((s == kind) & (h == chunk), i, 0), 0),
        )
        for kind in range(2)
        for chunk in range(CHUNKS)
    ]
    full = pltpu.HBM((1, HALF, COLS), F32)
    return pl.pallas_call(
        momentum_kernel,
        out_shape=[full, full],
        grid_spec=pltpu.PrefetchScalarGridSpec(
            num_scalar_prefetch=1,
            grid=(2, CHUNKS, n),
            in_specs=[whole] * 2 + terms,
            out_specs=[whole, whole],
        ),
        compiler_params=params(24),
        cost_estimate=cost(0, 11 * MB),
        name="momentum_step",
    )(where, km, vm, *own, *got)


def mean_kernel(where, pre, own, got, partner, *refs):
    nkw, nvw = refs[-2:]
    s = pl.program_id(0)

    def run(g):
        def body(rows):
            mean = 0.5 * ((pre[rows, :] - learn_rate * g[rows, :].astype(F32)) + partner[rows, :].astype(F32))
            nkw[0, rows, :] = mean[:, :COLS]
            nvw[0, rows, :] = mean[:, COLS:]

        by_rows(TILE, body)

    @pl.when(s == 0)
    def _():
        run(own)

    @pl.when(s == 1)
    def _():
        run(got)


def mean(where, chunk, pre, own, got, partner, before):
    grid, whole, term, moved = chunk_specs(chunk)
    full = pltpu.HBM((1, HALF, COLS), F32)
    extra = [] if before is None else list(before)
    return pl.pallas_call(
        mean_kernel,
        out_shape=[full, full],
        grid_spec=pltpu.PrefetchScalarGridSpec(
            num_scalar_prefetch=1,
            grid=grid,
            in_specs=[moved, term, term, moved] + [anywhere()] * len(extra),
            out_specs=[whole, whole],
        ),
        input_output_aliases={5: 0, 6: 1} if extra else {},
        compiler_params=params(24),
        cost_estimate=cost(0, 8 * MB),
        name="average",
    )(where, pre, own, got, partner, *extra)


def to_right(a):
    return lax.ppermute(a, "tensor", [(t, (t + 2) % 8) for t in range(8)])


def to_left(a):
    return lax.ppermute(a, "tensor", [(t, (t + 6) % 8) for t in range(8)])


def to_core(a):
    return lax.ppermute(a, "tensor", [(t, t ^ 1) for t in range(8)])


def to_z(a):
    return lax.ppermute(a, "fsdp", [(0, 1), (1, 0)])


def to_z_core(a):
    return lax.ppermute(a, ("fsdp", "tensor"), [(i, i ^ 9) for i in range(16)])


def to_partner(a, bit):
    n = lax.axis_size("gossip")
    return lax.ppermute(a, "gossip", [(i, i ^ (1 << bit)) for i in range(n)])


def after(value, *others):
    return lax.optimization_barrier((value, others))[0]


def exchange(bit, where, km, vm, kv, pre, terms, xs, w_own, w_core):
    own, send = weight_terms(0, kv, xs)
    got = to_core(send)
    moved = moved_chunk(pre[0], own, got)
    partner = to_partner(moved, bit)
    o_terms, s_terms = terms[:4], terms[4:]
    o_left = to_left(o_terms[2])
    o_relayed = o_terms[1] + to_right(o_terms[0])
    own1, send = weight_terms(1, after(kv, own), xs)
    got1 = to_core(send)
    p_own, p_send = projection(*xs, w_own, w_core)
    o_right = to_right(after(o_relayed, p_send))
    keep, p_send = projection_sum(p_own, to_core(p_send))
    p_z = to_z(p_send)
    partner1 = to_partner(after(moved_chunk(pre[1], own1, got1), keep), bit)
    keys, values = projection_end(where, keep, p_z)
    o_z, o_zc = sum3(o_terms[3], o_right, o_left)
    z, zc = to_z(o_z), to_z_core(o_zc)
    weights = mean(where, 0, pre[0], own, got, partner, None)
    s_left = to_left(after(s_terms[2] + to_left(after(s_terms[0], o_left)), o_z, weights[0]))
    s_right = to_right(after(s_terms[1], o_right, p_z if bit else p_send))
    momenta = momentum_step(after(where, o_z), km, vm, (own, own1), (got, got1))
    s_own, s_core = sum3(after(s_terms[3], momenta, weights), s_right, s_left)
    parts = (s_own, to_core(s_core), z, zc)
    if bit:
        input_grad = join(where, *parts)
        partner1 = after(partner1, input_grad)
    weights = mean(where, 1, pre[1], own1, got1, partner1, weights)
    if not bit:
        input_grad = join(where, *after(parts, weights[0]))
    return keys, values, input_grad, *weights, *momenta


def per_device(normed, kc, vc, kw, vw, km, vm, step_index):
    t = lax.axis_index("tensor")
    where = jnp.stack([lax.axis_index("fsdp"), t // 2, t % 2]).astype(jnp.int32)
    levels = lax.axis_size("gossip").bit_length() - 1
    bit = step_index % levels

    normed, kc, vc, kw, vw, km, vm = map(in_hbm, (normed, kc, vc, kw, vw, km, vm))
    kv_own, x_core, z_core, x_own, x_z = split_inputs(where, normed, kc, vc)
    x_core = to_core(x_core)
    a = jnp.concatenate([x_own, x_core], axis=0)
    b = jnp.concatenate([to_z(x_z), to_z_core(z_core)], axis=0)
    a3, a1 = to_right(a), to_left(a)
    w_own, w_send, *pre = prepare(after(where, a), kw, vw, km, vm)
    a3, b, w_own, w_send = lax.optimization_barrier((a3, b, w_own, w_send))
    a1, kv_own = lax.optimization_barrier((a1, kv_own))
    a2 = to_right(a3)
    kv_z = to_z(kv_own)
    b3, b1 = to_right(b), to_left(b)
    b2 = to_left(b1)
    kv = jnp.stack([kv_own.reshape(8, ROWS, 256), kv_z.reshape(8, ROWS, 256)], axis=1).reshape(1024, 256)
    kv = after(kv, a2)
    kv = order_cotangents(where, kv, to_core(kv))
    w_core = to_core(w_send)
    terms = input_terms(kv, w_own, w_core)
    xs = (a, b, a1, b1, a2, b2, a3, b3)
    kv = after(kv, terms[0])
    return lax.switch(
        bit,
        [partial(exchange, k) for k in range(levels)],
        where, km, vm, kv, pre, terms, xs, w_own, w_core,
    )


def solution(mesh):
    rows = P(("gossip", "fsdp", "tensor"), None)
    heads = P(("gossip", "fsdp"), "tensor")
    weight = P("gossip", "fsdp", "tensor")
    return jax.shard_map(
        per_device,
        mesh=mesh,
        in_specs=(rows, heads, heads, weight, weight, weight, weight, P()),
        out_specs=(heads, heads, rows, weight, weight, weight, weight),
        check_vma=False,
    )
```

```python
from functools import partial

import jax
import jax.numpy as jnp
from jax import lax
from jax.experimental import pallas as pl
from jax.experimental.pallas import tpu as pltpu
from jax.sharding import PartitionSpec as P

D = 8192
SCALING = D ** (-0.5)
momentum_decay = 0.9
learn_rate = 0.5

F32 = jnp.float32
BF = jnp.bfloat16
HALF = 4096
QUARTER = 2048
CHUNKS = 2
CH = QUARTER // CHUNKS
ROWS = 64
TOK = 512
COLS = 128
TILE = 1024

MB = 1024 * 1024


def sds(shape, dtype):
    return jax.ShapeDtypeStruct(shape, dtype)


def params(mib):
    return pltpu.CompilerParams(vmem_limit_bytes=mib * MB)


def cost(flops, nbytes):
    return pl.CostEstimate(flops=flops // 1000, bytes_accessed=nbytes // 1000, transcendentals=0)


def in_hbm(x):
    return pltpu.with_memory_space_constraint(x, pltpu.HBM)


def by_rows(rows, body, size=128):
    @pl.loop(0, rows // size)
    def _(i):
        body(pl.ds(pl.multiple_of(i * size, size), size))


def smem():
    return pl.BlockSpec(memory_space=pltpu.SMEM)


def vmem():
    return pl.BlockSpec(memory_space=pltpu.VMEM)


def copies(pairs, sems):
    started = [pltpu.make_async_copy(src, dst, sems.at[i]) for i, (src, dst) in enumerate(pairs)]
    for copy in started:
        copy.start()
    for copy in started:
        copy.wait()


def anywhere():
    return pl.BlockSpec(memory_space=pl.ANY)


def split_kernel(where, x, k, v, kv, core_own, core_other, own, other, sems):
    core = (core_own, core_other)
    f, c = where[0], where[2]
    pairs = []
    for g, out in enumerate((own, other)):
        q = 2 * (f + g - 2 * f * g)
        start = pl.multiple_of((q + 1 - c) * QUARTER, QUARTER)
        pairs.append((x.at[:, pl.ds(start, QUARTER)], core[g]))
        start = pl.multiple_of((q + c) * QUARTER, QUARTER)
        pairs.append((x.at[:, pl.ds(start, QUARTER)], out))
    pairs += [(k, kv.at[:, :COLS]), (v, kv.at[:, COLS:])]
    copies(pairs, sems)


def split_inputs(where, x, k, v):
    piece = sds((ROWS, QUARTER), BF)
    return pl.pallas_call(
        split_kernel,
        out_shape=[sds((TOK, 2 * COLS), BF), piece, piece, piece, piece],
        in_specs=[smem()] + [anywhere()] * 3,
        out_specs=[anywhere()] * 5,
        scratch_shapes=[pltpu.SemaphoreType.DMA((6,))],
        compiler_params=params(4),
        cost_estimate=cost(0, 2_600_000),
        name="split_inputs",
    )(where, x, k, v)


def prepare_kernel(where, kw, vw, km, vm, w_own, w_send, *pre):
    h, s = pl.program_id(0), pl.program_id(1)
    halves = ((kw, km, slice(0, COLS)), (vw, vm, slice(COLS, 2 * COLS)))
    for chunk in range(CHUNKS):
        for kind, rounded in ((0, w_own), (1, w_send)):

            @pl.when((h == chunk) & (s == kind))
            def _():
                def body(rows):
                    for w, m, cols in halves:
                        value = w[0, rows, :]
                        pre[chunk][rows, cols] = value - (learn_rate * momentum_decay) * m[0, rows, :]
                        rounded[rows, cols] = value.astype(BF)

                by_rows(TILE, body)


def prepare(where, kw, vw, km, vm):
    n = CH // TILE

    def at(h, s, i, w):
        q = s + w[2] - 2 * s * w[2]
        return (0, (q * CHUNKS + h) * n + i, 0)

    def chunk_at(chunk):
        def index(h, s, i, w):
            inside = s * n + i
            return (jnp.where(h == chunk, inside, jnp.where(h < chunk, 0, 2 * n - 1)), 0)

        return index

    whole = pl.BlockSpec((1, TILE, COLS), at)
    tile = (TILE, 256)
    return pl.pallas_call(
        prepare_kernel,
        out_shape=[sds((QUARTER, 256), BF)] * 2 + [sds((2 * CH, 256), F32)] * CHUNKS,
        grid_spec=pltpu.PrefetchScalarGridSpec(
            num_scalar_prefetch=1,
            grid=(CHUNKS, 2, n),
            in_specs=[whole] * 4,
            out_specs=[
                pl.BlockSpec(tile, lambda h, s, i, w: (h * n + jnp.where(s == 0, i, n - 1), 0)),
                pl.BlockSpec(tile, lambda h, s, i, w: (h * n + jnp.where(s == 1, i, 0), 0)),
            ]
            + [pl.BlockSpec(tile, chunk_at(chunk)) for chunk in range(CHUNKS)],
        ),
        compiler_params=params(24),
        cost_estimate=cost(0, 14 * MB),
        name="prepare_weights",
    )(where, kw, vw, km, vm)


def order_kernel(where, own, core, out):
    y, c = where[1], where[2]
    for j in range(4):
        for cr in range(2):
            t = 2 * lax.rem(y + j, 4) + (c + cr - 2 * c * cr)
            for g in range(2):
                row = pl.multiple_of(t * 2 * ROWS + g * ROWS, ROWS)
                to = j * 256 + g * 128 + cr * ROWS
                out[to : to + ROWS, : 2 * COLS] = own[pl.ds(row, ROWS), :]
                out[to : to + ROWS, 2 * COLS :] = core[pl.ds(row, ROWS), :]


def order_cotangents(where, own, core):
    return pl.pallas_call(
        order_kernel,
        out_shape=sds((1024, 512), BF),
        in_specs=[smem()] + [vmem()] * 2,
        out_specs=vmem(),
        compiler_params=params(8),
        cost_estimate=cost(0, 2 * MB),
        name="order_cotangents",
    )(where, own, core)


NT = (((1,), (1,)), ((), ()))
TN = (((0,), (0,)), ((), ()))
DXT = 1024


def dx_kernel(kv, w0, w1, *outs):
    part = lax.dot_general(kv[:, :256], w0[...], NT, preferred_element_type=F32)
    part += lax.dot_general(kv[:, 256:], w1[...], NT, preferred_element_type=F32)
    part = (part * SCALING).astype(BF)
    for g in range(2):
        for out, chip in zip(outs[4 * g : 4 * g + 4], (2, 1, 3, 0)):
            base = 256 * chip + 128 * (1 - g)
            out[...] = part[base : base + 128]


def input_terms(kv, w0, w1):
    spec = pl.BlockSpec((128, DXT), lambda i: (0, i))
    wspec = pl.BlockSpec((DXT, 256), lambda i: (i, 0))
    return pl.pallas_call(
        dx_kernel,
        out_shape=[sds((128, QUARTER), BF)] * 8,
        grid=(QUARTER // DXT,),
        in_specs=[pl.BlockSpec((1024, 512), lambda i: (0, 0)), wspec, wspec],
        out_specs=[spec] * 8,
        compiler_params=params(24),
        cost_estimate=cost(2 * 1024 * 512 * QUARTER, 7 * MB),
        name="input_terms",
    )(kv, w0, w1)


def dw_kernel(kv, *refs):
    xs, (own, send) = refs[:8], refs[8:]
    x = jnp.concatenate([r[...] for r in xs], axis=0)
    g = lax.dot_general(x, kv[...], TN, preferred_element_type=F32) * SCALING
    own[...] = g[:, :256]
    send[...] = g[:, 256:].astype(BF)


def weight_terms(chunk, kv, xs):
    t = 512
    n = CH // t
    return pl.pallas_call(
        dw_kernel,
        out_shape=[sds((CH, 256), F32), sds((CH, 256), BF)],
        grid=(n,),
        in_specs=[pl.BlockSpec((1024, 512), lambda i: (0, 0))]
        + [pl.BlockSpec((128, t), lambda i: (0, chunk * n + i))] * 8,
        out_specs=[pl.BlockSpec((t, 256), lambda i: (i, 0))] * 2,
        compiler_params=params(24),
        cost_estimate=cost(2 * 1024 * 512 * CH, 5 * MB),
        name="weight_terms",
    )(kv, *xs)


def proj_kernel(*refs):
    xs, (w0, w1), (own, send), acc = refs[:8], refs[8:10], refs[10:12], refs[12]
    i = pl.program_id(0)
    w = jnp.concatenate([w0[...], w1[...]], axis=1)

    @pl.when(i == 0)
    def _():
        acc[...] = jnp.zeros_like(acc)

    for k in range(8):
        rows = slice(128 * k, 128 * k + 128)
        acc[rows] += jnp.dot(xs[k][...], w, preferred_element_type=F32)

    @pl.when(i == pl.num_programs(0) - 1)
    def _():
        own[...] = acc[:, :256] * SCALING
        send[...] = (acc[:, 256:] * SCALING).astype(BF)


def projection(*args):
    t = 512
    wspec = pl.BlockSpec((t, 256), lambda i: (i, 0))
    return pl.pallas_call(
        proj_kernel,
        out_shape=[sds((1024, 256), F32), sds((1024, 256), BF)],
        grid=(QUARTER // t,),
        in_specs=[pl.BlockSpec((128, t), lambda i: (0, i))] * 8 + [wspec] * 2,
        out_specs=[pl.BlockSpec((1024, 256), lambda i: (0, 0))] * 2,
        scratch_shapes=[pltpu.VMEM((1024, 512), F32)],
        compiler_params=params(24),
        cost_estimate=cost(2 * 1024 * 512 * QUARTER, 8 * MB),
        name="projection",
    )(*args)


def proj_sum_kernel(own, got, keep, send):
    for at in range(0, 1024, 64):
        j, o, cr = at // 256, at // 128 % 2, at // 64 % 2
        far = at + 64 - 128 * cr
        total = own[at : at + 64] + got[far : far + 64].astype(F32)
        to = j * 128 + cr * 64
        if o:
            send[to : to + 64] = total.astype(BF)
        else:
            keep[to : to + 64] = total


def projection_sum(own, got):
    return pl.pallas_call(
        proj_sum_kernel,
        out_shape=[sds((512, 256), F32), sds((512, 256), BF)],
        in_specs=[vmem()] * 2,
        out_specs=[vmem()] * 2,
        compiler_params=params(8),
        cost_estimate=cost(0, 2 * MB),
        name="projection_sum",
    )(own, got)


def proj_end_kernel(where, keep, got, keys, values):
    y, c = where[1], where[2]
    for j in range(4):
        for cr in range(2):
            chip = lax.rem(y + j, 4)
            row = pl.multiple_of(chip * 2 * ROWS + (c + cr - 2 * c * cr) * ROWS, ROWS)
            at = j * 128 + cr * ROWS
            total = (keep[at : at + ROWS] + got[at : at + ROWS].astype(F32)).astype(BF)
            keys[pl.ds(row, ROWS), :] = total[:, :COLS]
            values[pl.ds(row, ROWS), :] = total[:, COLS:]


def projection_end(where, keep, got):
    out = pltpu.HBM((512, COLS), BF)
    return pl.pallas_call(
        proj_end_kernel,
        out_shape=[out, out],
        in_specs=[smem()] + [vmem()] * 2,
        out_specs=[vmem()] * 2,
        compiler_params=params(8),
        cost_estimate=cost(0, MB),
        name="projection_end",
    )(where, keep, got)


def sum3_kernel(a, b, c, lo, hi):
    for at, out in ((0, lo), (64, hi)):

        def body(rows):
            far = pl.ds(pl.multiple_of(rows.start + at, 16), rows.size)
            out[rows, :] = (a[far, :].astype(F32) + b[far, :].astype(F32) + c[far, :].astype(F32)).astype(BF)

        by_rows(64, body, 16)


def sum3(a, b, c):
    out = sds((64, QUARTER), BF)
    return pl.pallas_call(
        sum3_kernel,
        out_shape=[out, out],
        in_specs=[vmem()] * 3,
        out_specs=[vmem()] * 2,
        compiler_params=params(8),
        cost_estimate=cost(0, 2 * MB),
        name="sum_terms",
    )(a, b, c)


def join_kernel(where, own, core, z, zc, out):
    f, c = where[0], where[2]
    quarters = (2 * f + c, 2 * f + 1 - c, 2 * (1 - f) + c, 2 * (1 - f) + 1 - c)
    for q, ref in zip(quarters, (own, core, z, zc)):
        out[:, pl.ds(pl.multiple_of(q * QUARTER, QUARTER), QUARTER)] = ref[...]


def join(where, own, core, z, zc):
    return pl.pallas_call(
        join_kernel,
        out_shape=pltpu.HBM((ROWS, D), BF),
        in_specs=[smem()] + [vmem()] * 4,
        out_specs=vmem(),
        compiler_params=params(8),
        cost_estimate=cost(0, 2 * MB),
        name="join_input_grad",
    )(where, own, core, z, zc)


def chunk_specs(chunk):
    n = CH // TILE
    per_quarter = QUARTER // TILE

    def at(s, i, w):
        q = s + w[2] - 2 * s * w[2]
        return (0, q * per_quarter + chunk * n + i, 0)

    whole = pl.BlockSpec((1, TILE, COLS), at)
    term = pl.BlockSpec((TILE, 256), lambda s, i, w: (i, 0))
    moved = pl.BlockSpec((TILE, 256), lambda s, i, w: (s * n + i, 0))
    return (2, n), whole, term, moved


def moved_kernel(pre, own, got, moved):
    def body(rows):
        moved[rows, :] = (pre[rows, :] - learn_rate * own[rows, :]).astype(BF)
        far = pl.ds(pl.multiple_of(rows.start + CH, 128), rows.size)
        moved[far, :] = (pre[far, :] - learn_rate * got[rows, :].astype(F32)).astype(BF)

    by_rows(CH, body)


def moved_chunk(pre, own, got):
    return pl.pallas_call(
        moved_kernel,
        out_shape=sds((2 * CH, 256), BF),
        in_specs=[vmem()] * 3,
        out_specs=vmem(),
        compiler_params=params(8),
        cost_estimate=cost(0, 5 * MB),
        name="moved_weights",
    )(pre, own, got)


def last_moved_kernel(pre, own, got, moved, half):
    def body(rows):
        far = pl.ds(pl.multiple_of(rows.start + CH, 128), rows.size)
        for at, g in ((rows, own), (far, got)):
            value = pre[at, :] - learn_rate * g[rows, :].astype(F32)
            moved[at, :] = value.astype(BF)
            half[at, :] = 0.5 * value

    by_rows(CH, body)


def last_moved_chunk(pre, own, got):
    return pl.pallas_call(
        last_moved_kernel,
        out_shape=[sds((2 * CH, 256), BF), sds((2 * CH, 256), F32)],
        in_specs=[vmem()] * 3,
        out_specs=[vmem()] * 2,
        compiler_params=params(12),
        cost_estimate=cost(0, 7 * MB),
        name="last_moved_weights",
    )(pre, own, got)


def last_mean_kernel(where, half, partner, *refs):
    nkw, nvw = refs[-2:]

    def body(rows):
        mean = half[rows, :] + 0.5 * partner[rows, :].astype(F32)
        nkw[0, rows, :] = mean[:, :COLS]
        nvw[0, rows, :] = mean[:, COLS:]

    by_rows(TILE, body)


def last_mean(where, half, partner, before):
    grid, whole, term, moved = chunk_specs(CHUNKS - 1)
    full = pltpu.HBM((1, HALF, COLS), F32)
    return pl.pallas_call(
        last_mean_kernel,
        out_shape=[full, full],
        grid_spec=pltpu.PrefetchScalarGridSpec(
            num_scalar_prefetch=1,
            grid=grid,
            in_specs=[moved, moved, anywhere(), anywhere()],
            out_specs=[whole, whole],
        ),
        input_output_aliases={3: 0, 4: 1},
        compiler_params=params(24),
        cost_estimate=cost(0, 5 * MB),
        name="last_average",
    )(where, half, partner, *before)


def momentum_kernel(where, km, vm, *refs):
    own, got, (nkm, nvm) = refs[:CHUNKS], refs[CHUNKS : 2 * CHUNKS], refs[2 * CHUNKS :]
    s, h = pl.program_id(0), pl.program_id(1)

    def run(g):
        def body(rows):
            nkm[0, rows, :] = momentum_decay * km[0, rows, :] + g[rows, :COLS].astype(F32)
            nvm[0, rows, :] = momentum_decay * vm[0, rows, :] + g[rows, COLS:].astype(F32)

        by_rows(TILE, body)

    for chunk in range(CHUNKS):

        @pl.when((s == 0) & (h == chunk))
        def _():
            run(own[chunk])

        @pl.when((s == 1) & (h == chunk))
        def _():
            run(got[chunk])


def momentum_step(where, km, vm, own, got):
    n = CH // TILE

    def at(s, h, i, w):
        q = s + w[2] - 2 * s * w[2]
        return (0, (q * CHUNKS + h) * n + i, 0)

    whole = pl.BlockSpec((1, TILE, COLS), at)
    terms = [
        pl.BlockSpec(
            (TILE, 256),
            lambda s, h, i, w, kind=kind, chunk=chunk: (jnp.where((s == kind) & (h == chunk), i, 0), 0),
        )
        for kind in range(2)
        for chunk in range(CHUNKS)
    ]
    full = pltpu.HBM((1, HALF, COLS), F32)
    return pl.pallas_call(
        momentum_kernel,
        out_shape=[full, full],
        grid_spec=pltpu.PrefetchScalarGridSpec(
            num_scalar_prefetch=1,
            grid=(2, CHUNKS, n),
            in_specs=[whole] * 2 + terms,
            out_specs=[whole, whole],
        ),
        compiler_params=params(24),
        cost_estimate=cost(0, 11 * MB),
        name="momentum_step",
    )(where, km, vm, *own, *got)


def mean_kernel(where, pre, own, got, partner, *refs):
    nkw, nvw = refs[-2:]
    s = pl.program_id(0)

    def run(g):
        def body(rows):
            mean = 0.5 * ((pre[rows, :] - learn_rate * g[rows, :].astype(F32)) + partner[rows, :].astype(F32))
            nkw[0, rows, :] = mean[:, :COLS]
            nvw[0, rows, :] = mean[:, COLS:]

        by_rows(TILE, body)

    @pl.when(s == 0)
    def _():
        run(own)

    @pl.when(s == 1)
    def _():
        run(got)


def mean(where, chunk, pre, own, got, partner, before):
    grid, whole, term, moved = chunk_specs(chunk)
    full = pltpu.HBM((1, HALF, COLS), F32)
    extra = [] if before is None else list(before)
    return pl.pallas_call(
        mean_kernel,
        out_shape=[full, full],
        grid_spec=pltpu.PrefetchScalarGridSpec(
            num_scalar_prefetch=1,
            grid=grid,
            in_specs=[moved, term, term, moved] + [anywhere()] * len(extra),
            out_specs=[whole, whole],
        ),
        input_output_aliases={5: 0, 6: 1} if extra else {},
        compiler_params=params(24),
        cost_estimate=cost(0, 8 * MB),
        name="average",
    )(where, pre, own, got, partner, *extra)


def to_right(a):
    return lax.ppermute(a, "tensor", [(t, (t + 2) % 8) for t in range(8)])


def to_left(a):
    return lax.ppermute(a, "tensor", [(t, (t + 6) % 8) for t in range(8)])


def to_core(a):
    return lax.ppermute(a, "tensor", [(t, t ^ 1) for t in range(8)])


def to_z(a):
    return lax.ppermute(a, "fsdp", [(0, 1), (1, 0)])


def to_z_core(a):
    return lax.ppermute(a, ("fsdp", "tensor"), [(i, i ^ 9) for i in range(16)])


def to_partner(a, bit):
    n = lax.axis_size("gossip")
    return lax.ppermute(a, "gossip", [(i, i ^ (1 << bit)) for i in range(n)])


def after(value, *others):
    return lax.optimization_barrier((value, others))[0]


def exchange(bit, where, km, vm, kv, pre, terms, xs, w_own, w_core):
    own, send = weight_terms(0, kv, xs)
    got = to_core(send)
    moved = moved_chunk(pre[0], own, got)
    partner = to_partner(moved, bit)
    o_terms, s_terms = terms[:4], terms[4:]
    o_left = to_left(o_terms[2])
    o_relayed = o_terms[1] + to_right(o_terms[0])
    own1, send = weight_terms(1, after(kv, own), xs)
    got1 = to_core(send)
    p_own, p_send = projection(*xs, w_own, w_core)
    o_right = to_right(after(o_relayed, p_send))
    keep, p_send = projection_sum(p_own, to_core(p_send))
    p_z = to_z(p_send)
    last, half = last_moved_chunk(pre[1], own1, got1)
    partner1 = to_partner(after(last, keep), bit)
    keys, values = projection_end(where, keep, p_z)
    o_z, o_zc = sum3(o_terms[3], o_right, o_left)
    z, zc = to_z(o_z), to_z_core(o_zc)
    weights = mean(where, 0, pre[0], own, got, partner, None)
    s_left = to_left(after(s_terms[2] + to_left(after(s_terms[0], o_left)), o_z, weights[0]))
    s_right = to_right(after(s_terms[1], o_right, p_z if bit else p_send))
    momenta = momentum_step(after(where, o_z), km, vm, (own, own1), (got, got1))
    s_own, s_core = sum3(after(s_terms[3], momenta, weights), s_right, s_left)
    parts = (s_own, to_core(s_core), z, zc)
    if bit:
        input_grad = join(where, *parts)
        partner1 = after(partner1, input_grad)
    weights = last_mean(where, half, partner1, weights)
    if not bit:
        input_grad = join(where, *after(parts, weights[0]))
    return keys, values, input_grad, *weights, *momenta


def per_device(normed, kc, vc, kw, vw, km, vm, step_index):
    t = lax.axis_index("tensor")
    where = jnp.stack([lax.axis_index("fsdp"), t // 2, t % 2]).astype(jnp.int32)
    levels = lax.axis_size("gossip").bit_length() - 1
    bit = step_index % levels

    normed, kc, vc, kw, vw, km, vm = map(in_hbm, (normed, kc, vc, kw, vw, km, vm))
    kv_own, x_core, z_core, x_own, x_z = split_inputs(where, normed, kc, vc)
    x_core = to_core(x_core)
    a = jnp.concatenate([x_own, x_core], axis=0)
    b = jnp.concatenate([to_z(x_z), to_z_core(z_core)], axis=0)
    a3, a1 = to_right(a), to_left(a)
    w_own, w_send, *pre = prepare(after(where, a), kw, vw, km, vm)
    a3, b, w_own, w_send = lax.optimization_barrier((a3, b, w_own, w_send))
    a1, kv_own = lax.optimization_barrier((a1, kv_own))
    a2 = to_right(a3)
    kv_z = to_z(kv_own)
    b3, b1 = to_right(b), to_left(b)
    b2 = to_left(b1)
    kv = jnp.stack([kv_own.reshape(8, ROWS, 256), kv_z.reshape(8, ROWS, 256)], axis=1).reshape(1024, 256)
    kv = after(kv, a2)
    kv = order_cotangents(where, kv, to_core(kv))
    w_core = to_core(w_send)
    terms = input_terms(kv, w_own, w_core)
    xs = (a, b, a1, b1, a2, b2, a3, b3)
    kv = after(kv, terms[0])
    return lax.switch(
        bit,
        [partial(exchange, k) for k in range(levels)],
        where, km, vm, kv, pre, terms, xs, w_own, w_core,
    )


def solution(mesh):
    rows = P(("gossip", "fsdp", "tensor"), None)
    heads = P(("gossip", "fsdp"), "tensor")
    weight = P("gossip", "fsdp", "tensor")
    return jax.shard_map(
        per_device,
        mesh=mesh,
        in_specs=(rows, heads, heads, weight, weight, weight, weight, P()),
        out_specs=(heads, heads, rows, weight, weight, weight, weight),
        check_vma=False,
    )
```
